512 devices in a mesh: line: 8 (over x, core), chip: 16 (over z), layer: 4 (over y).
Axes of the slice: x: 4, y: 4, z: 16, core: 2. Of those that a mesh axis runs over, the one named last changes fastest.
Arguments:
- warmth_field: float32 [512, 64, 2048], P('line', 'layer', 'chip'), may hold values from -1.5 to 1.5
- power_input: float32 [512, 64, 2048], P('line', 'layer', 'chip'), may hold values from -24 to 24
- inertia_weight: float32 [512, 64, 2048], P('line', 'layer', 'chip'), may hold values from 0.0012207031 to 0.0048828125
- conductivity_lookup: float32 [8], replicated, may hold values from 2 to 40
- substance_label: int32 [512, 64, 2048], P('line', 'layer', 'chip'), may hold values from 0 to 7
Outputs:
- residual: float32 [512, 64, 2048], P('line', 'layer', 'chip')
- heat_rate: float32 [512, 64, 2048], P('line', 'layer', 'chip')
The draws below stay inside these ranges and needn't reach their ends.
All inputs are finite; a program needn't handle non-finite values.
Results may differ from the reference program's by a relative error of at most 0.0037.
Values sent between devices are 32-bit elements; how exact they have to be, the bound alone decides.
A program may use at most 64 MiB of HBM per device.

```python
import math
import jax
import jax.numpy as jnp
from jax import lax

MATS = 8
COLUMN_COUNT_I = 512
TIER_COUNT = 64
COLUMN_COUNT_J = 2048


def set_ends(values, key, low, top_value):
    index_at = [jax.random.randint(jax.random.fold_in(key, axis), (), 0, length) for axis, length in enumerate(values.shape)]
    widest = values.shape.index(max(values.shape))
    next_to = index_at[:widest] + [(index_at[widest] + 1) % values.shape[widest]] + index_at[widest + 1:]
    return values.at[tuple(index_at)].set(low).at[tuple(next_to)].set(top_value)


def shard_levels(rng, dims, split, low, high):
    def one(axis_at, parts):
        heights = jax.random.uniform(jax.random.fold_in(jax.random.fold_in(rng, 6), axis_at), (parts,), jnp.float32, low / len(split), high / len(split))
        return jnp.repeat(jnp.exp(heights), dims[axis_at] // parts).reshape((-1,) + (1,) * (len(dims) - axis_at - 1))

    loudness = one(*split[0])
    for cut in split[1:]:
        loudness = loudness * one(*cut)
    return loudness


def normal_values(stream_key, extent, width, bound, cuts=(), held_as=jnp.bfloat16):
    array = jax.random.normal(stream_key, extent, jnp.float32) * width
    if len(cuts) > 0:
        array = shard_levels(stream_key, extent, cuts, -0.22, 0.18) * array
    return jnp.clip(array, min=-bound, max=bound).astype(held_as)


def setup_inputs(seed: int = 0) -> dict:
    seeds = jax.random.split(jax.random.key(seed), 6)
    warmth_field = normal_values(seeds[0], (COLUMN_COUNT_I, TIER_COUNT, COLUMN_COUNT_J), 0.1, 1.5, ((0, 8), (1, 4), (2, 16)), jnp.float32)
    power_input = normal_values(seeds[1], (COLUMN_COUNT_I, TIER_COUNT, COLUMN_COUNT_J), 4.0, 24.0, ((0, 8), (1, 4), (2, 16)), jnp.float32)
    inertia_weight = jnp.clip(jnp.exp(math.log(0.0048828125) - 1.3862944 * jax.random.uniform(seeds[2], (COLUMN_COUNT_I, TIER_COUNT, COLUMN_COUNT_J), jnp.float32) ** shard_levels(seeds[2], (COLUMN_COUNT_I, TIER_COUNT, COLUMN_COUNT_J), ((0, 8), (1, 4), (2, 16)), -0.2, 0.2)), 0.0012207031, 0.0048828125)
    conductivity_lookup = jnp.clip(jnp.exp(jax.random.uniform(seeds[3], (MATS,), jnp.float32, math.log(2.0), math.log(40.0))), 2.0, 40.0)
    substance_label = set_ends(jax.random.randint(seeds[4], (COLUMN_COUNT_I, TIER_COUNT, COLUMN_COUNT_J), 0, MATS), jax.random.fold_in(seeds[4], 1), 0, MATS - 1).astype(jnp.int32)
    return {"warmth_field": warmth_field, "power_input": power_input, "inertia_weight": inertia_weight, "conductivity_lookup": conductivity_lookup, "substance_label": substance_label}


def conductance(first, second):
    return 2.0 * first * second / jnp.maximum(first + second, 1e-30)


def reference(warmth_field, power_input, inertia_weight, conductivity_lookup, substance_label):
    coupling_strength = conductivity_lookup[substance_label]
    cond_pad = jnp.pad(coupling_strength, 1)
    bordered_warmth = jnp.pad(warmth_field, 1)
    shifts = [
        (slice(2, None), slice(1, -1), slice(1, -1)),
        (slice(None, -2), slice(1, -1), slice(1, -1)),
        (slice(1, -1), slice(2, None), slice(1, -1)),
        (slice(1, -1), slice(None, -2), slice(1, -1)),
        (slice(1, -1), slice(1, -1), slice(2, None)),
        (slice(1, -1), slice(1, -1), slice(None, -2)),
    ]
    energy_current = jnp.zeros_like(warmth_field)
    faces = []
    for choose_by_predicate in shifts:
        interface_average = conductance(coupling_strength, cond_pad[choose_by_predicate])
        faces.append(interface_average)
        energy_current = energy_current + interface_average * (warmth_field - bordered_warmth[choose_by_predicate])
    topmost_boundary_flag = (jnp.arange(TIER_COUNT) == TIER_COUNT - 1)[None, :, None]
    energy_current = energy_current + jnp.where(topmost_boundary_flag, coupling_strength * warmth_field, 0.0)
    residual = power_input - energy_current
    rhs = lax.optimization_barrier(residual.astype(jnp.bfloat16)).astype(jnp.float32)
    gplus = faces[0]
    gminus = faces[1]
    lower = -gminus
    upper = -gplus
    diag = inertia_weight + gminus + gplus

    def forward(carry, row):
        prev_c, prev_d = carry
        low, up, dia, right = row
        denom = dia - low * prev_c
        new_c = up / denom
        new_d = (right - low * prev_d) / denom
        return (new_c, new_d), (new_c, new_d)

    initial_shift = jnp.zeros(warmth_field.shape[1:], jnp.float32)
    _, (coef_c, coef_d) = lax.scan(forward, (initial_shift, initial_shift), (lower, upper, diag, rhs))

    def backward(after, row):
        cc, dd = row
        value = dd - cc * after
        return value, value

    _, correction = lax.scan(backward, initial_shift, (coef_c, coef_d), reverse=True)
    return residual, inertia_weight * correction
```

```python
import functools

import jax
import jax.numpy as jnp
from jax import lax
from jax.experimental import pallas as pl
from jax.experimental.pallas import tpu as pltpu
from jax.sharding import PartitionSpec as P

MESH = pl.DeviceIdType.MESH
RUNS = 8
STEPS = 8
F32 = jnp.float32


def recip(x):
    y = pltpu.reciprocal(x, approx=True)
    return y * (2.0 - x * y)


def conductance(first, second):
    return 2.0 * first * second * recip(first + second)


def eliminate(left, ground, right):
    inv = recip(left + ground + right)
    return left * inv, right * inv, inv


def spot(run, step):
    return pl.ds((run * STEPS + step) * 16, 16)


def read(ref, step):
    return jnp.stack([ref[spot(run, step), :] for run in range(RUNS)])


def write(ref, step, value):
    for run in range(RUNS):
        ref[spot(run, step), :] = value[run]


def kernel(
    count_line, count_chip, count_layer,
    temp_hbm, power_hbm, weight_hbm, lut, label_hbm,
    res_hbm, heat_hbm,
    temp, power, weight, label, cond, res, heat,
    gx, coef_t, coef_u, coef_q,
    line_send, line_recv, layer_send, layer_recv, chip_send, chip_recv,
    mats, rights,
    in_sem, out_sem, halo_send_sem, halo_recv_sem,
    mat_send_sem, mat_recv_sem, rhs_send_sem, rhs_recv_sem,
):
    line = lax.axis_index("line")
    chip = lax.axis_index("chip")
    layer = lax.axis_index("layer")
    depth, width = 16, 128

    loads = [
        pltpu.make_async_copy(src, dst, in_sem.at[n])
        for n, (src, dst) in enumerate(
            ((label_hbm, label), (temp_hbm, temp), (power_hbm, power), (weight_hbm, weight))
        )
    ]
    for load in loads:
        load.start()

    line_recv[...] = jnp.zeros_like(line_recv)
    layer_recv[...] = jnp.zeros_like(layer_recv)
    chip_recv[...] = jnp.zeros_like(chip_recv)

    has = (
        line > 0, line < count_line - 1,
        layer > 0, layer < count_layer - 1,
        chip > 0, chip < count_chip - 1,
    )
    where = (
        {"line": line - 1}, {"line": line + 1},
        {"layer": layer - 1}, {"layer": layer + 1},
        {"chip": chip - 1}, {"chip": chip + 1},
    )
    sends = (line_send, line_send, layer_send, layer_send, chip_send, chip_send)
    recvs = (line_recv, line_recv, layer_recv, layer_recv, chip_recv, chip_recv)

    barrier = pltpu.get_barrier_semaphore()
    peers = [lax.rem(line + r, count_line) for r in range(1, count_line)]
    for peer in peers:
        pl.semaphore_signal(barrier, inc=1, device_id={"line": peer}, device_id_type=MESH)
    for side in range(2, 6):
        @pl.when(has[side])
        def _():
            pl.semaphore_signal(barrier, inc=1, device_id=where[side], device_id_type=MESH)

    def halo(side):
        return pltpu.make_async_remote_copy(
            src_ref=sends[side] if side >= 4 else sends[side].at[side % 2],
            dst_ref=recvs[side].at[1 - side % 2],
            send_sem=halo_send_sem.at[side],
            recv_sem=halo_recv_sem.at[side - side % 2 + 1 - side % 2],
            device_id=where[side],
            device_id_type=MESH,
        )

    def halo_start(side):
        @pl.when(has[side])
        def _():
            halo(side).start()

    def halo_landed(side):
        @pl.when(has[side])
        def _():
            pltpu.make_async_remote_copy(
                src_ref=sends[side] if side >= 4 else sends[side].at[side % 2],
                dst_ref=recvs[side].at[side % 2],
                send_sem=halo_send_sem.at[side],
                recv_sem=halo_recv_sem.at[side],
                device_id=where[side],
                device_id_type=MESH,
            ).wait_recv()

    values = [lut[n] for n in range(8)]
    loads[0].wait()

    def look_up(tags):
        odd = (tags & 1) == 1
        two = (tags & 2) == 2
        four = tags >= 4
        pairs = [jnp.where(odd, values[2 * n + 1], values[2 * n]) for n in range(4)]
        halves = [jnp.where(two, pairs[2 * n + 1], pairs[2 * n]) for n in range(2)]
        return jnp.where(four, halves[1], halves[0])

    for i in range(STEPS):
        write(cond, i, look_up(label[:, i]))
    loads[1].wait()
    start, stop = spot(0, 0), spot(RUNS - 1, STEPS - 1)
    line_send[0, 0] = temp[start, :]
    line_send[0, 1] = cond[start, :]
    line_send[1, 0] = temp[stop, :]
    line_send[1, 1] = cond[stop, :]
    rows = RUNS * STEPS
    for end, first in ((0, 0), (1, depth - 1)):
        layer_send[end, 0] = temp[pl.ds(first, rows, stride=depth), :]
        layer_send[end, 1] = cond[pl.ds(first, rows, stride=depth), :]

    total = count_line - 1 + sum(side.astype(jnp.int32) for side in has[2:])
    pl.semaphore_wait(barrier, total)
    for side in range(4):
        halo_start(side)

    lane = lax.broadcasted_iota(jnp.int32, (1, 1, width), 2)
    packed = jnp.zeros((RUNS, depth, width), F32)
    for i in range(STEPS):
        packed = jnp.where(
            lane // 2 == 2 * i, pltpu.roll(read(temp, i), 4 * i + 1, 2),
            jnp.where(lane // 2 == 2 * i + 1, pltpu.roll(read(cond, i), 4 * i + 3, 2), packed),
        )
    packed = packed.reshape(2, 4, depth, width)
    dense = packed[:, 0]
    for k in range(1, 4):
        dense = jnp.where(lane // 32 == k, pltpu.roll(packed[:, k], 32 * k, 2), dense)
    chip_send[...] = dense
    halo_start(4)
    halo_start(5)

    loads[2].wait()
    row = lax.broadcasted_iota(jnp.int32, (1, depth, 1), 1)
    for i in range(STEPS):
        heat_here, k_here = read(temp, i), read(cond, i)
        flow_y = jnp.where(
            lane == width - 1, 0.0,
            conductance(k_here, pltpu.roll(k_here, width - 1, 2))
            * (heat_here - pltpu.roll(heat_here, width - 1, 2)),
        )
        flow_z = jnp.where(
            row == depth - 1, 0.0,
            conductance(k_here, pltpu.roll(k_here, depth - 1, 1))
            * (heat_here - pltpu.roll(heat_here, depth - 1, 1)),
        )
        write(res, i, (
            power[:, i]
            - (flow_y - pltpu.roll(flow_y, 1, 2))
            - (flow_z - pltpu.roll(flow_z, 1, 1))
        ))

    halo_landed(0)
    halo_landed(1)
    first_t, first_k = temp[start, :], cond[start, :]
    last_t, last_k = temp[stop, :], cond[stop, :]
    g_left = conductance(first_k, line_recv[0, 1])
    g_right = conductance(last_k, line_recv[1, 1])
    flow_left = g_left * (line_recv[0, 0] - first_t)
    flow_right = g_right * (last_t - line_recv[1, 0])
    flow = None
    for i in range(STEPS):
        heat_here, k_here = read(temp, i), read(cond, i)
        if i < STEPS - 1:
            g = conductance(k_here, read(cond, i + 1))
            flow_on = g * (heat_here - read(temp, i + 1))
        else:
            next_k = jnp.concatenate([read(cond, 0)[1:], line_recv[1:2, 1]], axis=0)
            next_t = jnp.concatenate([read(temp, 0)[1:], line_recv[1:2, 0]], axis=0)
            g = conductance(k_here, next_k)
            flow_on = g * (heat_here - next_t)
        gx[:, i] = g
        if i == 0:
            write(res, i, read(res, i) - flow_on)
        else:
            write(res, i, read(res, i) + flow - flow_on)
        flow = flow_on
    write(res, 0, read(res, 0) + jnp.concatenate([flow_left[None], flow[:-1]], axis=0))

    loads[3].wait()
    ya, c, yb = weight[:, 0], gx[:, 0], weight[:, 1]
    for i in range(1, STEPS - 1):
        u, t, inv = eliminate(c, yb, gx[:, i])
        ya = ya + u * yb
        c = c * t
        yb = weight[:, i + 1] + t * yb
        coef_u[:, i] = u
        coef_t[:, i] = t
        coef_q[:, i] = inv
    join = gx[:, STEPS - 1]
    tree = []
    while ya.shape[0] > 1:
        half = ya.shape[0] // 2
        ya_l, ya_r = (ya.reshape(half, 2, depth, width)[:, n] for n in range(2))
        yb_l, yb_r = (yb.reshape(half, 2, depth, width)[:, n] for n in range(2))
        c_l, c_r = (c.reshape(half, 2, depth, width)[:, n] for n in range(2))
        g, join = (join.reshape(half, 2, depth, width)[:, n] for n in range(2))
        first = eliminate(c_l, yb_l, g)
        u, t, _ = first
        ya = ya_l + u * yb_l
        c = c_l * t
        mid = ya_r + t * yb_l
        second = eliminate(c, mid, c_r)
        u, t, _ = second
        ya = ya + u * mid
        c = c * t
        yb = yb_r + t * mid
        tree.append((first, second))
    mats[line, 0] = ya[0]
    mats[line, 1] = c[0]
    mats[line, 2] = yb[0]
    mats[line, 3] = g_left

    def spread(block, send_sem, recv_sem):
        return [
            pltpu.make_async_remote_copy(
                src_ref=block.at[line],
                dst_ref=block.at[line],
                send_sem=send_sem.at[r],
                recv_sem=recv_sem.at[r],
                device_id={"line": peer},
                device_id_type=MESH,
            )
            for r, peer in enumerate(peers)
        ]

    def landed(block, send_sem, recv_sem):
        for r in range(count_line - 1):
            source = lax.rem(line + count_line - 1 - r, count_line)
            pltpu.make_async_remote_copy(
                src_ref=block.at[source],
                dst_ref=block.at[source],
                send_sem=send_sem.at[r],
                recv_sem=recv_sem.at[r],
                device_id={"line": source},
                device_id_type=MESH,
            ).wait_recv()

    mat_copies = spread(mats, mat_send_sem, mat_recv_sem)
    for copy in mat_copies:
        copy.start()

    halo_landed(2)
    halo_landed(3)
    is_top = layer == count_layer - 1
    for end, first in ((0, 0), (1, depth - 1)):
        own_t, own_k = layer_send[end, 0], layer_send[end, 1]
        g = conductance(own_k, layer_recv[end, 1])
        if end == 1:
            g = jnp.where(is_top, own_k, g)
        face = pl.ds(first, rows, stride=depth)
        res[face, :] = res[face, :] - g * (own_t - layer_recv[end, 0])

    halo_landed(4)
    halo_landed(5)
    own = chip_send[...]
    other = jnp.where(
        lane % 2 == 0, pltpu.roll(chip_recv[1], width - 1, 2), pltpu.roll(chip_recv[0], 1, 2)
    )
    edge = jnp.where(
        lane % 4 < 2,
        conductance(pltpu.roll(own, width - 2, 2), pltpu.roll(other, width - 2, 2))
        * (own - other),
        0.0,
    )
    edges = jnp.stack(
        [edge] + [pltpu.roll(edge, width - 32 * k, 2) for k in range(1, 4)], axis=1
    ).reshape(RUNS, depth, width)
    at_edge = (lane == 0) | (lane == width - 1)
    rounded = []
    for i in range(STEPS):
        total_res = read(res, i) - jnp.where(
            at_edge, pltpu.roll(edges, width - 1 - 4 * i, 2), 0.0
        )
        write(res, i, total_res)
        right = total_res.astype(jnp.bfloat16).astype(F32)
        if i == 0:
            ra = right
        elif i == 1:
            rb = right
        else:
            ra = ra + coef_u[:, i - 1] * rb
            held = coef_t[:, i - 1] * rb
            coef_q[:, i - 1] = coef_q[:, i - 1] * rb
            rb = right + held
    res_copy = pltpu.make_async_copy(res, res_hbm, out_sem.at[0])
    res_copy.start()

    held = []
    for (u1, t1, inv1), (u2, t2, inv2) in tree:
        half = ra.shape[0] // 2
        ra_l, ra_r = (ra.reshape(half, 2, depth, width)[:, n] for n in range(2))
        rb_l, rb_r = (rb.reshape(half, 2, depth, width)[:, n] for n in range(2))
        mid = ra_r + t1 * rb_l
        held.append((inv1 * rb_l, inv2 * mid))
        ra = ra_l + u1 * rb_l + u2 * mid
        rb = rb_r + t2 * mid
    rights[line, 0] = ra[0]
    rights[line, 1] = rb[0]
    rhs_copies = spread(rights, rhs_send_sem, rhs_recv_sem)
    for copy in rhs_copies:
        copy.start()

    landed(mats, mat_send_sem, mat_recv_sem)
    zero = jnp.zeros((depth, width), F32)
    before, after = zero, zero
    up, down = [], []
    for j in range(count_line - 1):
        a, b, cc = mats[j, 0], mats[j, 2], mats[j, 1]
        if j > 0:
            g = mats[j, 3]
            v = g * recip(g + before)
            a = a + v * before
        else:
            v = zero
        u = cc * recip(a + cc)
        before = jnp.where(j < line, b + u * a, before)
        up.append((u, v))
        n = count_line - 1 - j
        a, b, cc = mats[n, 0], mats[n, 2], mats[n, 1]
        if j > 0:
            g = mats[n + 1, 3]
            v = g * recip(g + after)
            b = b + v * after
        else:
            v = zero
        u = cc * recip(b + cc)
        after = jnp.where(n > line, a + u * b, after)
        down.append((u, v))
    ya, c, yb = ya[0], c[0], yb[0]
    v_left = jnp.where(line > 0, g_left * recip(g_left + before + 1e-30), 0.0)
    v_right = jnp.where(
        line < count_line - 1, g_right * recip(g_right + after + 1e-30), 0.0
    )
    a = ya + v_left * before
    b = yb + v_right * after
    inv = recip(a * b + c * (a + b))
    from_a, from_b, cross = (b + c) * inv, (a + c) * inv, c * inv

    landed(rights, rhs_send_sem, rhs_recv_sem)
    left_in, right_in = zero, zero
    for j in range(count_line - 1):
        u, v = up[j]
        new = rights[j, 1] + u * (rights[j, 0] + v * left_in)
        left_in = jnp.where(j < line, new, left_in)
        n = count_line - 1 - j
        u, v = down[j]
        new = rights[n, 0] + u * (rights[n, 1] + v * right_in)
        right_in = jnp.where(n > line, new, right_in)
    ra = ra[0] + v_left * left_in
    rb = rb[0] + v_right * right_in
    xa = (from_a * ra + cross * rb)[None]
    xb = (cross * ra + from_b * rb)[None]

    for ((u1, t1, _), (u2, t2, _)), (q1, q2) in zip(reversed(tree), reversed(held)):
        xr = q2 + u2 * xa + t2 * xb
        xl = q1 + u1 * xa + t1 * xr
        size = 2 * xa.shape[0]
        xa = jnp.stack([xa, xr], axis=1).reshape(size, depth, width)
        xb = jnp.stack([xl, xb], axis=1).reshape(size, depth, width)
    heat[:, 0] = weight[:, 0] * xa
    heat[:, STEPS - 1] = weight[:, STEPS - 1] * xb
    x = xb
    for i in range(STEPS - 2, 0, -1):
        x = coef_q[:, i] + coef_u[:, i] * xa + coef_t[:, i] * x
        heat[:, i] = weight[:, i] * x
    heat_copy = pltpu.make_async_copy(heat, heat_hbm, out_sem.at[1])
    heat_copy.start()

    for side in range(6):
        @pl.when(has[side])
        def _():
            halo(side).wait_send()
    for copy in mat_copies + rhs_copies:
        copy.wait_send()
    res_copy.wait()
    heat_copy.wait()


def shards(counts, warmth_field, power_input, inertia_weight, conductivity_lookup, substance_label):
    depth, width = warmth_field.shape[1:]
    shape = (RUNS, STEPS, depth, width)
    vmem = pltpu.VMEM
    whole = vmem(shape, F32)
    others = counts[0] - 1
    dma = pltpu.SemaphoreType.DMA
    any_space = pl.BlockSpec(memory_space=pl.ANY)
    flat = (RUNS * STEPS * depth, width)
    rows = vmem(flat, F32)
    residual, heat_rate = pl.pallas_call(
        functools.partial(kernel, *counts),
        out_shape=(jax.ShapeDtypeStruct(flat, F32), jax.ShapeDtypeStruct(shape, F32)),
        in_specs=[any_space, any_space, any_space, pl.BlockSpec(memory_space=pltpu.SMEM), any_space],
        out_specs=(any_space, any_space),
        scratch_shapes=[
            rows, whole, whole, vmem(shape, jnp.int32), rows, rows, whole,
            whole, whole, whole, whole,
            vmem((2, 2, depth, width), F32), vmem((2, 2, depth, width), F32),
            vmem((2, 2, RUNS * STEPS, width), F32), vmem((2, 2, RUNS * STEPS, width), F32),
            vmem((2, depth, width), F32), vmem((2, 2, depth, width), F32),
            vmem((counts[0], 4, depth, width), F32), vmem((counts[0], 2, depth, width), F32),
            dma((4,)), dma((2,)), dma((6,)), dma((6,)),
            dma((others,)), dma((others,)), dma((others,)), dma((others,)),
        ],
        compiler_params=pltpu.CompilerParams(
            collective_id=0, has_side_effects=True, vmem_limit_bytes=32 * 1024 * 1024
        ),
    )(
        warmth_field.reshape(flat), power_input.reshape(shape), inertia_weight.reshape(shape),
        conductivity_lookup, substance_label.reshape(shape),
    )
    return residual.reshape(warmth_field.shape), heat_rate.reshape(warmth_field.shape)


def solution(mesh):
    counts = tuple(mesh.shape[axis] for axis in ("line", "chip", "layer"))
    spec = P("line", "layer", "chip")
    return jax.shard_map(
        functools.partial(shards, counts),
        mesh=mesh,
        in_specs=(spec, spec, spec, P(), spec),
        out_specs=(spec, spec),
        check_vma=False,
    )
```

```python
import functools

import jax
import jax.numpy as jnp
from jax import lax
from jax.experimental import pallas as pl
from jax.experimental.pallas import tpu as pltpu
from jax.sharding import PartitionSpec as P

MESH = pl.DeviceIdType.MESH
RUNS = 8
STEPS = 8
F32 = jnp.float32


def recip(x):
    y = pltpu.reciprocal(x, approx=True)
    return y * (2.0 - x * y)


def conductance(first, second):
    return 2.0 * first * second * recip(first + second)


def eliminate(left, ground, right):
    inv = recip(left + ground + right)
    return left * inv, right * inv, inv


def spot(run, step):
    return pl.ds((run * STEPS + step) * 16, 16)


def read(ref, step):
    return jnp.stack([ref[spot(run, step), :] for run in range(RUNS)])


def write(ref, step, value):
    for run in range(RUNS):
        ref[spot(run, step), :] = value[run]


def kernel(
    count_line, count_chip, count_layer,
    temp_hbm, power_hbm, weight_hbm, lut_hbm, label_hbm,
    res, heat,
    temp, power, weight, label, lut, cond,
    gx, coef_t, coef_u, coef_q,
    line_send, line_recv, layer_send, layer_recv, chip_send, chip_recv,
    mats, rights,
    in_sem, halo_send_sem, halo_recv_sem,
    mat_send_sem, mat_recv_sem, rhs_send_sem, rhs_recv_sem,
):
    line = lax.axis_index("line")
    chip = lax.axis_index("chip")
    layer = lax.axis_index("layer")
    depth, width = 16, 128

    loads = [
        pltpu.make_async_copy(src, dst, in_sem.at[n])
        for n, (src, dst) in enumerate(
            (
                (label_hbm, label), (temp_hbm, temp), (power_hbm, power),
                (weight_hbm, weight), (lut_hbm, lut),
            )
        )
    ]
    for n in (4, 0, 1, 2, 3):
        loads[n].start()

    line_recv[...] = jnp.zeros_like(line_recv)
    layer_recv[...] = jnp.zeros_like(layer_recv)
    chip_recv[...] = jnp.zeros_like(chip_recv)

    has = (
        line > 0, line < count_line - 1,
        layer > 0, layer < count_layer - 1,
        chip > 0, chip < count_chip - 1,
    )
    where = (
        {"line": line - 1}, {"line": line + 1},
        {"layer": layer - 1}, {"layer": layer + 1},
        {"chip": chip - 1}, {"chip": chip + 1},
    )
    sends = (line_send, line_send, layer_send, layer_send, chip_send, chip_send)
    recvs = (line_recv, line_recv, layer_recv, layer_recv, chip_recv, chip_recv)

    barrier = pltpu.get_barrier_semaphore()
    peers = [lax.rem(line + r, count_line) for r in range(1, count_line)]
    for peer in peers:
        pl.semaphore_signal(barrier, inc=1, device_id={"line": peer}, device_id_type=MESH)
    for side in range(2, 6):
        @pl.when(has[side])
        def _():
            pl.semaphore_signal(barrier, inc=1, device_id=where[side], device_id_type=MESH)

    def halo(side):
        return pltpu.make_async_remote_copy(
            src_ref=sends[side] if side >= 4 else sends[side].at[side % 2],
            dst_ref=recvs[side].at[1 - side % 2],
            send_sem=halo_send_sem.at[side],
            recv_sem=halo_recv_sem.at[side - side % 2 + 1 - side % 2],
            device_id=where[side],
            device_id_type=MESH,
        )

    def halo_start(side):
        @pl.when(has[side])
        def _():
            halo(side).start()

    def halo_landed(side):
        @pl.when(has[side])
        def _():
            pltpu.make_async_remote_copy(
                src_ref=sends[side] if side >= 4 else sends[side].at[side % 2],
                dst_ref=recvs[side].at[side % 2],
                send_sem=halo_send_sem.at[side],
                recv_sem=halo_recv_sem.at[side],
                device_id=where[side],
                device_id_type=MESH,
            ).wait_recv()

    loads[4].wait()
    values = [lut[n] for n in range(8)]
    loads[0].wait()

    def look_up(tags):
        odd = (tags & 1) == 1
        two = (tags & 2) == 2
        four = tags >= 4
        pairs = [jnp.where(odd, values[2 * n + 1], values[2 * n]) for n in range(4)]
        halves = [jnp.where(two, pairs[2 * n + 1], pairs[2 * n]) for n in range(2)]
        return jnp.where(four, halves[1], halves[0])

    for i in range(STEPS):
        write(cond, i, look_up(label[:, i]))
    loads[1].wait()
    start, stop = spot(0, 0), spot(RUNS - 1, STEPS - 1)
    line_send[0, 0] = temp[start, :]
    line_send[0, 1] = cond[start, :]
    line_send[1, 0] = temp[stop, :]
    line_send[1, 1] = cond[stop, :]
    rows = RUNS * STEPS
    for end, first in ((0, 0), (1, depth - 1)):
        layer_send[end, 0] = temp[pl.ds(first, rows, stride=depth), :]
        layer_send[end, 1] = cond[pl.ds(first, rows, stride=depth), :]

    total = count_line - 1 + sum(side.astype(jnp.int32) for side in has[2:])
    pl.semaphore_wait(barrier, total)
    for side in range(4):
        halo_start(side)

    lane = lax.broadcasted_iota(jnp.int32, (1, 1, width), 2)
    packed = jnp.zeros((RUNS, depth, width), F32)
    for i in range(STEPS):
        packed = jnp.where(
            lane // 2 == 2 * i, pltpu.roll(read(temp, i), 4 * i + 1, 2),
            jnp.where(lane // 2 == 2 * i + 1, pltpu.roll(read(cond, i), 4 * i + 3, 2), packed),
        )
    packed = packed.reshape(2, 4, depth, width)
    dense = packed[:, 0]
    for k in range(1, 4):
        dense = jnp.where(lane // 32 == k, pltpu.roll(packed[:, k], 32 * k, 2), dense)
    chip_send[...] = dense
    halo_start(4)
    halo_start(5)

    loads[2].wait()
    row = lax.broadcasted_iota(jnp.int32, (1, depth, 1), 1)
    for i in range(STEPS):
        heat_here, k_here = read(temp, i), read(cond, i)
        flow_y = jnp.where(
            lane == width - 1, 0.0,
            conductance(k_here, pltpu.roll(k_here, width - 1, 2))
            * (heat_here - pltpu.roll(heat_here, width - 1, 2)),
        )
        flow_z = jnp.where(
            row == depth - 1, 0.0,
            conductance(k_here, pltpu.roll(k_here, depth - 1, 1))
            * (heat_here - pltpu.roll(heat_here, depth - 1, 1)),
        )
        write(res, i, (
            power[:, i]
            - (flow_y - pltpu.roll(flow_y, 1, 2))
            - (flow_z - pltpu.roll(flow_z, 1, 1))
        ))

    halo_landed(0)
    halo_landed(1)
    first_t, first_k = temp[start, :], cond[start, :]
    last_t, last_k = temp[stop, :], cond[stop, :]
    g_left = conductance(first_k, line_recv[0, 1])
    g_right = conductance(last_k, line_recv[1, 1])
    flow_left = g_left * (line_recv[0, 0] - first_t)
    flow_right = g_right * (last_t - line_recv[1, 0])
    flow = None
    for i in range(STEPS):
        heat_here, k_here = read(temp, i), read(cond, i)
        if i < STEPS - 1:
            g = conductance(k_here, read(cond, i + 1))
            flow_on = g * (heat_here - read(temp, i + 1))
        else:
            next_k = jnp.concatenate([read(cond, 0)[1:], line_recv[1:2, 1]], axis=0)
            next_t = jnp.concatenate([read(temp, 0)[1:], line_recv[1:2, 0]], axis=0)
            g = conductance(k_here, next_k)
            flow_on = g * (heat_here - next_t)
        gx[:, i] = g
        if i == 0:
            write(res, i, read(res, i) - flow_on)
        else:
            write(res, i, read(res, i) + flow - flow_on)
        flow = flow_on
    write(res, 0, read(res, 0) + jnp.concatenate([flow_left[None], flow[:-1]], axis=0))

    loads[3].wait()
    ya, c, yb = weight[:, 0], gx[:, 0], weight[:, 1]
    for i in range(1, STEPS - 1):
        u, t, inv = eliminate(c, yb, gx[:, i])
        ya = ya + u * yb
        c = c * t
        yb = weight[:, i + 1] + t * yb
        coef_u[:, i] = u
        coef_t[:, i] = t
        coef_q[:, i] = inv
    join = gx[:, STEPS - 1]
    tree = []
    while ya.shape[0] > 1:
        half = ya.shape[0] // 2
        ya_l, ya_r = (ya.reshape(half, 2, depth, width)[:, n] for n in range(2))
        yb_l, yb_r = (yb.reshape(half, 2, depth, width)[:, n] for n in range(2))
        c_l, c_r = (c.reshape(half, 2, depth, width)[:, n] for n in range(2))
        g, join = (join.reshape(half, 2, depth, width)[:, n] for n in range(2))
        first = eliminate(c_l, yb_l, g)
        u, t, _ = first
        ya = ya_l + u * yb_l
        c = c_l * t
        mid = ya_r + t * yb_l
        second = eliminate(c, mid, c_r)
        u, t, _ = second
        ya = ya + u * mid
        c = c * t
        yb = yb_r + t * mid
        tree.append((first, second))
    mats[line, 0] = ya[0]
    mats[line, 1] = c[0]
    mats[line, 2] = yb[0]
    mats[line, 3] = g_left

    def spread(block, send_sem, recv_sem):
        return [
            pltpu.make_async_remote_copy(
                src_ref=block.at[line],
                dst_ref=block.at[line],
                send_sem=send_sem.at[r],
                recv_sem=recv_sem.at[r],
                device_id={"line": peer},
                device_id_type=MESH,
            )
            for r, peer in enumerate(peers)
        ]

    def landed(block, send_sem, recv_sem):
        for r in range(count_line - 1):
            source = lax.rem(line + count_line - 1 - r, count_line)
            pltpu.make_async_remote_copy(
                src_ref=block.at[source],
                dst_ref=block.at[source],
                send_sem=send_sem.at[r],
                recv_sem=recv_sem.at[r],
                device_id={"line": source},
                device_id_type=MESH,
            ).wait_recv()

    mat_copies = spread(mats, mat_send_sem, mat_recv_sem)
    for copy in mat_copies:
        copy.start()

    halo_landed(2)
    halo_landed(3)
    is_top = layer == count_layer - 1
    for end, first in ((0, 0), (1, depth - 1)):
        own_t, own_k = layer_send[end, 0], layer_send[end, 1]
        g = conductance(own_k, layer_recv[end, 1])
        if end == 1:
            g = jnp.where(is_top, own_k, g)
        face = pl.ds(first, rows, stride=depth)
        res[face, :] = res[face, :] - g * (own_t - layer_recv[end, 0])

    halo_landed(4)
    halo_landed(5)
    own = chip_send[...]
    other = jnp.where(
        lane % 2 == 0, pltpu.roll(chip_recv[1], width - 1, 2), pltpu.roll(chip_recv[0], 1, 2)
    )
    edge = jnp.where(
        lane % 4 < 2,
        conductance(pltpu.roll(own, width - 2, 2), pltpu.roll(other, width - 2, 2))
        * (own - other),
        0.0,
    )
    edges = jnp.stack(
        [edge] + [pltpu.roll(edge, width - 32 * k, 2) for k in range(1, 4)], axis=1
    ).reshape(RUNS, depth, width)
    at_edge = (lane == 0) | (lane == width - 1)
    rounded = []
    for i in range(STEPS):
        total_res = read(res, i) - jnp.where(
            at_edge, pltpu.roll(edges, width - 1 - 4 * i, 2), 0.0
        )
        write(res, i, total_res)
        right = total_res.astype(jnp.bfloat16).astype(F32)
        if i == 0:
            ra = right
        elif i == 1:
            rb = right
        else:
            ra = ra + coef_u[:, i - 1] * rb
            held = coef_t[:, i - 1] * rb
            coef_q[:, i - 1] = coef_q[:, i - 1] * rb
            rb = right + held

    held = []
    for (u1, t1, inv1), (u2, t2, inv2) in tree:
        half = ra.shape[0] // 2
        ra_l, ra_r = (ra.reshape(half, 2, depth, width)[:, n] for n in range(2))
        rb_l, rb_r = (rb.reshape(half, 2, depth, width)[:, n] for n in range(2))
        mid = ra_r + t1 * rb_l
        held.append((inv1 * rb_l, inv2 * mid))
        ra = ra_l + u1 * rb_l + u2 * mid
        rb = rb_r + t2 * mid
    rights[line, 0] = ra[0]
    rights[line, 1] = rb[0]
    rhs_copies = spread(rights, rhs_send_sem, rhs_recv_sem)
    for copy in rhs_copies:
        copy.start()

    landed(mats, mat_send_sem, mat_recv_sem)
    zero = jnp.zeros((depth, width), F32)
    before, after = zero, zero
    up, down = [], []
    for j in range(count_line - 1):
        a, b, cc = mats[j, 0], mats[j, 2], mats[j, 1]
        if j > 0:
            g = mats[j, 3]
            v = g * recip(g + before)
            a = a + v * before
        else:
            v = zero
        u = cc * recip(a + cc)
        before = jnp.where(j < line, b + u * a, before)
        up.append((u, v))
        n = count_line - 1 - j
        a, b, cc = mats[n, 0], mats[n, 2], mats[n, 1]
        if j > 0:
            g = mats[n + 1, 3]
            v = g * recip(g + after)
            b = b + v * after
        else:
            v = zero
        u = cc * recip(b + cc)
        after = jnp.where(n > line, a + u * b, after)
        down.append((u, v))
    ya, c, yb = ya[0], c[0], yb[0]
    v_left = jnp.where(line > 0, g_left * recip(g_left + before + 1e-30), 0.0)
    v_right = jnp.where(
        line < count_line - 1, g_right * recip(g_right + after + 1e-30), 0.0
    )
    a = ya + v_left * before
    b = yb + v_right * after
    inv = recip(a * b + c * (a + b))
    from_a, from_b, cross = (b + c) * inv, (a + c) * inv, c * inv

    landed(rights, rhs_send_sem, rhs_recv_sem)
    left_in, right_in = zero, zero
    for j in range(count_line - 1):
        u, v = up[j]
        new = rights[j, 1] + u * (rights[j, 0] + v * left_in)
        left_in = jnp.where(j < line, new, left_in)
        n = count_line - 1 - j
        u, v = down[j]
        new = rights[n, 0] + u * (rights[n, 1] + v * right_in)
        right_in = jnp.where(n > line, new, right_in)
    ra = ra[0] + v_left * left_in
    rb = rb[0] + v_right * right_in
    xa = (from_a * ra + cross * rb)[None]
    xb = (cross * ra + from_b * rb)[None]

    for ((u1, t1, _), (u2, t2, _)), (q1, q2) in zip(reversed(tree), reversed(held)):
        xr = q2 + u2 * xa + t2 * xb
        xl = q1 + u1 * xa + t1 * xr
        size = 2 * xa.shape[0]
        xa = jnp.stack([xa, xr], axis=1).reshape(size, depth, width)
        xb = jnp.stack([xl, xb], axis=1).reshape(size, depth, width)
    heat[:, 0] = weight[:, 0] * xa
    heat[:, STEPS - 1] = weight[:, STEPS - 1] * xb
    x = xb
    for i in range(STEPS - 2, 0, -1):
        x = coef_q[:, i] + coef_u[:, i] * xa + coef_t[:, i] * x
        heat[:, i] = weight[:, i] * x

    for side in range(6):
        @pl.when(has[side])
        def _():
            halo(side).wait_send()
    for copy in mat_copies + rhs_copies:
        copy.wait_send()


def store(res, heat, res_hbm, heat_hbm, sem):
    copies = [
        pltpu.make_async_copy(res, res_hbm, sem.at[0]),
        pltpu.make_async_copy(heat, heat_hbm, sem.at[1]),
    ]
    for copy in copies:
        copy.start()
    for copy in copies:
        copy.wait()


def shards(counts, warmth_field, power_input, inertia_weight, conductivity_lookup, substance_label):
    depth, width = warmth_field.shape[1:]
    shape = (RUNS, STEPS, depth, width)
    vmem = pltpu.VMEM
    whole = vmem(shape, F32)
    others = counts[0] - 1
    dma = pltpu.SemaphoreType.DMA
    hbm_space = pl.BlockSpec(memory_space=pltpu.HBM)
    vmem_space = pl.BlockSpec(memory_space=pltpu.VMEM)
    flat = (RUNS * STEPS * depth, width)
    rows = vmem(flat, F32)
    residual, heat_rate = pl.pallas_call(
        functools.partial(kernel, *counts),
        out_shape=(rows, whole),
        in_specs=[hbm_space] * 5,
        out_specs=(vmem_space, vmem_space),
        scratch_shapes=[
            rows, whole, whole, vmem(shape, jnp.int32), pltpu.SMEM((8,), F32), rows,
            whole, whole, whole, whole,
            vmem((2, 2, depth, width), F32), vmem((2, 2, depth, width), F32),
            vmem((2, 2, RUNS * STEPS, width), F32), vmem((2, 2, RUNS * STEPS, width), F32),
            vmem((2, depth, width), F32), vmem((2, 2, depth, width), F32),
            vmem((counts[0], 4, depth, width), F32), vmem((counts[0], 2, depth, width), F32),
            dma((5,)), dma((6,)), dma((6,)),
            dma((others,)), dma((others,)), dma((others,)), dma((others,)),
        ],
        compiler_params=pltpu.CompilerParams(
            collective_id=0, has_side_effects=True, vmem_limit_bytes=32 * 1024 * 1024
        ),
    )(
        *(
            pltpu.with_memory_space_constraint(operand, pltpu.HBM)
            for operand in (
                warmth_field.reshape(flat), power_input.reshape(shape),
                inertia_weight.reshape(shape), conductivity_lookup,
                substance_label.reshape(shape),
            )
        )
    )
    residual, heat_rate = pl.pallas_call(
        store,
        out_shape=(jax.ShapeDtypeStruct(flat, F32), jax.ShapeDtypeStruct(shape, F32)),
        in_specs=[pl.BlockSpec(memory_space=pl.ANY)] * 2,
        out_specs=(hbm_space, hbm_space),
        scratch_shapes=[dma((2,))],
    )(
        pltpu.with_memory_space_constraint(residual, pltpu.VMEM),
        pltpu.with_memory_space_constraint(heat_rate, pltpu.VMEM),
    )
    return residual.reshape(warmth_field.shape), heat_rate.reshape(warmth_field.shape)


def solution(mesh):
    counts = tuple(mesh.shape[axis] for axis in ("line", "chip", "layer"))
    spec = P("line", "layer", "chip")
    return jax.shard_map(
        functools.partial(shards, counts),
        mesh=mesh,
        in_specs=(spec, spec, spec, P(), spec),
        out_specs=(spec, spec),
        check_vma=False,
    )
```

```python
import functools

import jax
import jax.numpy as jnp
from jax import lax
from jax.experimental import pallas as pl
from jax.experimental.pallas import tpu as pltpu
from jax.sharding import PartitionSpec as P

MESH = pl.DeviceIdType.MESH
RUNS = 8
STEPS = 8
F32 = jnp.float32


def recip(x):
    y = pltpu.reciprocal(x, approx=True)
    return y * (2.0 - x * y)


def conductance(first, second):
    return 2.0 * first * second * recip(first + second)


def eliminate(left, ground, right):
    inv = recip(left + ground + right)
    return left * inv, right * inv, inv


def spot(run, step):
    return pl.ds((run * STEPS + step) * 16, 16)


def read(ref, step):
    return jnp.stack([ref[spot(run, step), :] for run in range(RUNS)])


def write(ref, step, value):
    for run in range(RUNS):
        ref[spot(run, step), :] = value[run]


def kernel(
    count_line, count_chip, count_layer,
    temp_hbm, power_hbm, weight_hbm, lut_hbm, label_hbm,
    res, heat,
    temp, power, weight, label, lut, cond,
    gx, coef_t, coef_u, coef_q,
    line_send, line_recv, layer_send, layer_recv, chip_send, chip_recv,
    mats, rights,
    in_sem, halo_send_sem, halo_recv_sem,
    mat_send_sem, mat_recv_sem, rhs_send_sem, rhs_recv_sem,
):
    line = lax.axis_index("line")
    chip = lax.axis_index("chip")
    layer = lax.axis_index("layer")
    depth, width = 16, 128
    rows = RUNS * STEPS

    has = (
        line > 0, line < count_line - 1,
        layer > 0, layer < count_layer - 1,
        chip > 0, chip < count_chip - 1,
    )
    where = (
        {"line": line - 1}, {"line": line + 1},
        {"layer": layer - 1}, {"layer": layer + 1},
        {"chip": chip - 1}, {"chip": chip + 1},
    )
    sends = (line_send, line_send, layer_send, layer_send, chip_send, chip_send)
    recvs = (line_recv, line_recv, layer_recv, layer_recv, chip_recv, chip_recv)

    other = line + 1 - 2 * lax.rem(line, 2)
    offsets = [4, 2, count_line - 2]
    peers = [lax.rem(core + step, count_line) for step in offsets for core in (line, other)] + [other]
    sources = [peers[n] for n in (0, 1, 4, 5, 2, 3, 6)]

    barrier = pltpu.get_barrier_semaphore()
    for side in range(2, 6):
        @pl.when(has[side])
        def _():
            pl.semaphore_signal(barrier, inc=1, device_id=where[side], device_id_type=MESH)
    for peer in peers[2:] + peers[:2]:
        pl.semaphore_signal(barrier, inc=1, device_id={"line": peer}, device_id_type=MESH)

    loads = [
        pltpu.make_async_copy(src, dst, in_sem.at[n])
        for n, (src, dst) in enumerate(
            (
                (label_hbm, label), (temp_hbm, temp), (lut_hbm, lut),
                (weight_hbm, weight), (power_hbm, power),
            )
        )
    ]
    for load in loads:
        load.start()

    for side in range(6):
        @pl.when(jnp.logical_not(has[side]))
        def _():
            recvs[side][side % 2] = jnp.zeros(recvs[side].shape[1:], F32)

    def halo(side):
        return pltpu.make_async_remote_copy(
            src_ref=sends[side] if side >= 4 else sends[side].at[side % 2],
            dst_ref=recvs[side].at[1 - side % 2],
            send_sem=halo_send_sem.at[side],
            recv_sem=halo_recv_sem.at[side - side % 2 + 1 - side % 2],
            device_id=where[side],
            device_id_type=MESH,
        )

    def halo_start(side):
        @pl.when(has[side])
        def _():
            halo(side).start()

    def halo_landed(side):
        @pl.when(has[side])
        def _():
            pltpu.make_async_remote_copy(
                src_ref=sends[side] if side >= 4 else sends[side].at[side % 2],
                dst_ref=recvs[side].at[side % 2],
                send_sem=halo_send_sem.at[side],
                recv_sem=halo_recv_sem.at[side],
                device_id=where[side],
                device_id_type=MESH,
            ).wait_recv()

    loads[0].wait()
    loads[1].wait()
    start, stop = spot(0, 0), spot(RUNS - 1, STEPS - 1)
    for end, face in ((0, start), (1, stop)):
        line_send[end, 0] = temp[face, :]
        line_send[end, 1] = label[face, :].astype(F32)
    for end, first in ((0, 0), (1, depth - 1)):
        face = pl.ds(first, rows, stride=depth)
        layer_send[end, 0] = temp[face, :]
        layer_send[end, 1] = label[face, :].astype(F32)

    lane = lax.broadcasted_iota(jnp.int32, (1, 1, width), 2)
    packed = jnp.zeros((RUNS, depth, width), F32)
    for i in range(STEPS):
        packed = jnp.where(
            lane // 2 == 2 * i, pltpu.roll(read(temp, i), 4 * i + 1, 2),
            jnp.where(
                lane // 2 == 2 * i + 1,
                pltpu.roll(read(label, i).astype(F32), 4 * i + 3, 2),
                packed,
            ),
        )
    packed = packed.reshape(2, 4, depth, width)
    dense = packed[:, 0]
    for k in range(1, 4):
        dense = jnp.where(lane // 32 == k, pltpu.roll(packed[:, k], 32 * k, 2), dense)
    chip_send[...] = dense

    total = count_line - 1 + sum(side.astype(jnp.int32) for side in has[2:])
    pl.semaphore_wait(barrier, total)
    for side in (4, 5, 2, 3, 0, 1):
        halo_start(side)

    loads[2].wait()
    values = [lut[n] for n in range(8)]

    def look_up(tags):
        odd = (tags & 1) == 1
        two = (tags & 2) == 2
        four = tags >= 4
        pairs = [jnp.where(odd, values[2 * n + 1], values[2 * n]) for n in range(4)]
        halves = [jnp.where(two, pairs[2 * n + 1], pairs[2 * n]) for n in range(2)]
        return jnp.where(four, halves[1], halves[0])

    def face_look_up(tags):
        return look_up(tags.astype(jnp.int32))

    for i in range(STEPS):
        write(cond, i, look_up(read(label, i)))

    for i in range(STEPS - 1):
        gx[:, i] = conductance(read(cond, i), read(cond, i + 1))
    k_last, k_first = read(cond, STEPS - 1), read(cond, 0)
    join = conductance(k_last, jnp.concatenate([k_first[1:], k_first[:1]], axis=0))
    gx[:, STEPS - 1] = join

    loads[3].wait()
    ya, c, yb = weight[:, 0], gx[:, 0], weight[:, 1]
    for i in range(1, STEPS - 1):
        u, t, inv = eliminate(c, yb, gx[:, i])
        ya = ya + u * yb
        c = c * t
        yb = weight[:, i + 1] + t * yb
        coef_u[:, i] = u
        coef_t[:, i] = t
        coef_q[:, i] = inv
    tree = []
    while ya.shape[0] > 1:
        half = ya.shape[0] // 2
        ya_l, ya_r = (ya.reshape(half, 2, depth, width)[:, n] for n in range(2))
        yb_l, yb_r = (yb.reshape(half, 2, depth, width)[:, n] for n in range(2))
        c_l, c_r = (c.reshape(half, 2, depth, width)[:, n] for n in range(2))
        g, join = (join.reshape(half, 2, depth, width)[:, n] for n in range(2))
        first = eliminate(c_l, yb_l, g)
        u, t, _ = first
        ya = ya_l + u * yb_l
        c = c_l * t
        mid = ya_r + t * yb_l
        second = eliminate(c, mid, c_r)
        u, t, _ = second
        ya = ya + u * mid
        c = c * t
        yb = yb_r + t * mid
        tree.append((first, second))
    ya, c, yb = ya[0], c[0], yb[0]
    t_a, u_a, inv_a = eliminate(2.0 * k_first[0], ya, c)
    y_left, yb, c = t_a * ya, yb + u_a * ya, t_a * c
    u_b, t_b, inv_b = eliminate(c, yb, 2.0 * k_last[RUNS - 1])
    y_left, y_right, c = y_left + u_b * yb, t_b * yb, c * t_b
    mats[line, 0] = y_left
    mats[line, 1] = c
    mats[line, 2] = y_right

    def spread(block, send_sem, recv_sem):
        return [
            pltpu.make_async_remote_copy(
                src_ref=block.at[line],
                dst_ref=block.at[line],
                send_sem=send_sem.at[n],
                recv_sem=recv_sem.at[n],
                device_id={"line": peer},
                device_id_type=MESH,
            )
            for n, peer in enumerate(peers)
        ]

    def landed(block, send_sem, recv_sem):
        for n, source in enumerate(sources):
            pltpu.make_async_remote_copy(
                src_ref=block.at[source],
                dst_ref=block.at[source],
                send_sem=send_sem.at[n],
                recv_sem=recv_sem.at[n],
                device_id={"line": source},
                device_id_type=MESH,
            ).wait_recv()

    mat_copies = spread(mats, mat_send_sem, mat_recv_sem)
    for copy in mat_copies:
        copy.start()

    loads[4].wait()
    row = lax.broadcasted_iota(jnp.int32, (1, depth, 1), 1)
    flow = None
    for i in range(STEPS):
        heat_here, k_here = read(temp, i), read(cond, i)
        flow_y = jnp.where(
            lane == width - 1, 0.0,
            conductance(k_here, pltpu.roll(k_here, width - 1, 2))
            * (heat_here - pltpu.roll(heat_here, width - 1, 2)),
        )
        flow_z = jnp.where(
            row == depth - 1, 0.0,
            conductance(k_here, pltpu.roll(k_here, depth - 1, 1))
            * (heat_here - pltpu.roll(heat_here, depth - 1, 1)),
        )
        part = (
            power[:, i]
            - (flow_y - pltpu.roll(flow_y, 1, 2))
            - (flow_z - pltpu.roll(flow_z, 1, 1))
        )
        if i < STEPS - 1:
            flow_on = gx[:, i] * (heat_here - read(temp, i + 1))
        else:
            flow_on = gx[:-1, i] * (heat_here[:-1] - read(temp, 0)[1:])
            flow_on = jnp.concatenate([flow_on, jnp.zeros((1, depth, width), F32)], axis=0)
        if i > 0:
            part = part + flow
        write(res, i, part - flow_on)
        flow = flow_on
    for run in range(1, RUNS):
        here = spot(run, 0)
        res[here, :] = res[here, :] + flow[run - 1]

    halo_landed(0)
    halo_landed(1)
    for end, face in ((0, start), (1, stop)):
        g = conductance(cond[face, :], face_look_up(line_recv[end, 1]))
        g = jnp.where(has[end], g, 0.0)
        res[face, :] = res[face, :] - g * (temp[face, :] - line_recv[end, 0])
    halo_landed(2)
    halo_landed(3)
    is_top = layer == count_layer - 1
    for end, first in ((0, 0), (1, depth - 1)):
        face = pl.ds(first, rows, stride=depth)
        own_k = cond[face, :]
        g = conductance(own_k, face_look_up(layer_recv[end, 1]))
        if end == 0:
            g = jnp.where(has[2], g, 0.0)
        else:
            g = jnp.where(is_top, own_k, g)
        res[face, :] = res[face, :] - g * (layer_send[end, 0] - layer_recv[end, 0])

    own = chip_send[...]
    own_k = face_look_up(pltpu.roll(own, width - 2, 2))
    halo_landed(4)
    halo_landed(5)
    beside = jnp.where(
        lane % 2 == 0, pltpu.roll(chip_recv[1], width - 1, 2), pltpu.roll(chip_recv[0], 1, 2)
    )
    beside_k = face_look_up(pltpu.roll(beside, width - 2, 2))
    open_lane = ((lane % 4 == 0) & has[5]) | ((lane % 4 == 1) & has[4])
    edge = jnp.where(open_lane, conductance(own_k, beside_k) * (own - beside), 0.0)
    edges = jnp.stack(
        [edge] + [pltpu.roll(edge, width - 32 * k, 2) for k in range(1, 4)], axis=1
    ).reshape(RUNS, depth, width)
    at_edge = (lane == 0) | (lane == width - 1)
    for i in range(STEPS):
        total_res = read(res, i) - jnp.where(
            at_edge, pltpu.roll(edges, width - 1 - 4 * i, 2), 0.0
        )
        write(res, i, total_res)
        right = total_res.astype(jnp.bfloat16).astype(F32)
        if i == 0:
            ra = right
        elif i == 1:
            rb = right
        else:
            ra = ra + coef_u[:, i - 1] * rb
            held = coef_t[:, i - 1] * rb
            coef_q[:, i - 1] = coef_q[:, i - 1] * rb
            rb = right + held

    held = []
    for (u1, t1, inv1), (u2, t2, inv2) in tree:
        half = ra.shape[0] // 2
        ra_l, ra_r = (ra.reshape(half, 2, depth, width)[:, n] for n in range(2))
        rb_l, rb_r = (rb.reshape(half, 2, depth, width)[:, n] for n in range(2))
        mid = ra_r + t1 * rb_l
        held.append((inv1 * rb_l, inv2 * mid))
        ra = ra_l + u1 * rb_l + u2 * mid
        rb = rb_r + t2 * mid
    ra, rb = ra[0], rb[0]
    rb = rb + u_a * ra
    r_left, r_right = t_a * ra + u_b * rb, t_b * rb
    rights[line, 0] = r_left
    rights[line, 1] = r_right
    rhs_copies = spread(rights, rhs_send_sem, rhs_recv_sem)
    for copy in rhs_copies:
        copy.start()
    q_a, q_b = inv_a * ra, inv_b * rb

    landed(mats, mat_send_sem, mat_recv_sem)
    zero = jnp.zeros((depth, width), F32)
    before, after = zero, zero
    up, down = [], []
    for j in range(count_line - 1):
        a = before + mats[j, 0]
        u = mats[j, 1] * recip(a + mats[j, 1])
        before = jnp.where(j < line, mats[j, 2] + u * a, before)
        up.append(u)
        n = count_line - 1 - j
        a = after + mats[n, 2]
        u = mats[n, 1] * recip(a + mats[n, 1])
        after = jnp.where(n > line, mats[n, 0] + u * a, after)
        down.append(u)
    a = y_left + before
    b = y_right + after
    inv = recip(a * b + c * (a + b))
    from_a, from_b, cross = (b + c) * inv, (a + c) * inv, c * inv

    landed(rights, rhs_send_sem, rhs_recv_sem)
    left_in, right_in = zero, zero
    for j in range(count_line - 1):
        new = rights[j, 1] + up[j] * (rights[j, 0] + left_in)
        left_in = jnp.where(j < line, new, left_in)
        n = count_line - 1 - j
        new = rights[n, 0] + down[j] * (rights[n, 1] + right_in)
        right_in = jnp.where(n > line, new, right_in)
    left_in = left_in + r_left
    right_in = right_in + r_right
    x_left = from_a * left_in + cross * right_in
    x_right = cross * left_in + from_b * right_in
    xb = q_b + u_b * x_left + t_b * x_right
    xa = q_a + t_a * x_left + u_a * xb
    xa, xb = xa[None], xb[None]

    for ((u1, t1, _), (u2, t2, _)), (q1, q2) in zip(reversed(tree), reversed(held)):
        xr = q2 + u2 * xa + t2 * xb
        xl = q1 + u1 * xa + t1 * xr
        size = 2 * xa.shape[0]
        xa = jnp.stack([xa, xr], axis=1).reshape(size, depth, width)
        xb = jnp.stack([xl, xb], axis=1).reshape(size, depth, width)
    heat[:, 0] = weight[:, 0] * xa
    heat[:, STEPS - 1] = weight[:, STEPS - 1] * xb
    x = xb
    for i in range(STEPS - 2, 0, -1):
        x = coef_q[:, i] + coef_u[:, i] * xa + coef_t[:, i] * x
        heat[:, i] = weight[:, i] * x

    for side in range(6):
        @pl.when(has[side])
        def _():
            halo(side).wait_send()
    for copy in mat_copies + rhs_copies:
        copy.wait_send()


def store(res, heat, res_hbm, heat_hbm, sem):
    copies = [
        pltpu.make_async_copy(res, res_hbm, sem.at[0]),
        pltpu.make_async_copy(heat, heat_hbm, sem.at[1]),
    ]
    for copy in copies:
        copy.start()
    for copy in copies:
        copy.wait()


def shards(counts, warmth_field, power_input, inertia_weight, conductivity_lookup, substance_label):
    depth, width = warmth_field.shape[1:]
    shape = (RUNS, STEPS, depth, width)
    vmem = pltpu.VMEM
    whole = vmem(shape, F32)
    others = counts[0] - 1
    dma = pltpu.SemaphoreType.DMA
    hbm_space = pl.BlockSpec(memory_space=pltpu.HBM)
    vmem_space = pl.BlockSpec(memory_space=pltpu.VMEM)
    flat = (RUNS * STEPS * depth, width)
    rows = vmem(flat, F32)
    residual, heat_rate = pl.pallas_call(
        functools.partial(kernel, *counts),
        out_shape=(rows, whole),
        in_specs=[hbm_space] * 5,
        out_specs=(vmem_space, vmem_space),
        scratch_shapes=[
            rows, whole, whole, vmem(flat, jnp.int32), pltpu.SMEM((8,), F32), rows,
            whole, whole, whole, whole,
            vmem((2, 2, depth, width), F32), vmem((2, 2, depth, width), F32),
            vmem((2, 2, RUNS * STEPS, width), F32), vmem((2, 2, RUNS * STEPS, width), F32),
            vmem((2, depth, width), F32), vmem((2, 2, depth, width), F32),
            vmem((counts[0], 3, depth, width), F32), vmem((counts[0], 2, depth, width), F32),
            dma((5,)), dma((6,)), dma((6,)),
            dma((others,)), dma((others,)), dma((others,)), dma((others,)),
        ],
        compiler_params=pltpu.CompilerParams(
            collective_id=0, has_side_effects=True, vmem_limit_bytes=32 * 1024 * 1024
        ),
    )(
        *(
            pltpu.with_memory_space_constraint(operand, pltpu.HBM)
            for operand in (
                warmth_field.reshape(flat), power_input.reshape(shape),
                inertia_weight.reshape(shape), conductivity_lookup,
                substance_label.reshape(flat),
            )
        )
    )
    residual, heat_rate = pl.pallas_call(
        store,
        out_shape=(jax.ShapeDtypeStruct(flat, F32), jax.ShapeDtypeStruct(shape, F32)),
        in_specs=[pl.BlockSpec(memory_space=pl.ANY)] * 2,
        out_specs=(hbm_space, hbm_space),
        scratch_shapes=[dma((2,))],
    )(
        pltpu.with_memory_space_constraint(residual, pltpu.VMEM),
        pltpu.with_memory_space_constraint(heat_rate, pltpu.VMEM),
    )
    return residual.reshape(warmth_field.shape), heat_rate.reshape(warmth_field.shape)


def solution(mesh):
    counts = tuple(mesh.shape[axis] for axis in ("line", "chip", "layer"))
    spec = P("line", "layer", "chip")
    return jax.shard_map(
        functools.partial(shards, counts),
        mesh=mesh,
        in_specs=(spec, spec, spec, P(), spec),
        out_specs=(spec, spec),
        check_vma=False,
    )
```

```python
import functools

import jax
import jax.numpy as jnp
from jax import lax
from jax.experimental import pallas as pl
from jax.experimental.pallas import tpu as pltpu
from jax.sharding import PartitionSpec as P

MESH = pl.DeviceIdType.MESH
RUNS = 8
STEPS = 8
F32 = jnp.float32


def recip(x):
    y = pltpu.reciprocal(x, approx=True)
    return y * (2.0 - x * y)


def conductance(first, second):
    return 2.0 * first * second * recip(first + second)


def eliminate(left, ground, right):
    inv = recip(left + ground + right)
    return left * inv, right * inv, inv


def spot(run, step):
    return pl.ds((run * STEPS + step) * 16, 16)


def read(ref, step):
    return jnp.stack([ref[spot(run, step), :] for run in range(RUNS)])


def write(ref, step, value):
    for run in range(RUNS):
        ref[spot(run, step), :] = value[run]


def kernel(
    count_line, count_chip, count_layer,
    temp_hbm, power_hbm, weight_hbm, lut_hbm, label_hbm,
    res, heat,
    temp, power, weight, label, lut, cond,
    gx, coef_t, coef_u, coef_q,
    line_send, line_recv, layer_send, layer_recv, chip_send, chip_recv,
    mats, rights,
    in_sem, halo_send_sem, halo_recv_sem,
    mat_send_sem, mat_recv_sem, rhs_send_sem, rhs_recv_sem, ready_sem,
):
    line = lax.axis_index("line")
    chip = lax.axis_index("chip")
    layer = lax.axis_index("layer")
    depth, width = 16, 128
    rows = RUNS * STEPS

    has = (
        line > 0, line < count_line - 1,
        layer > 0, layer < count_layer - 1,
        chip > 0, chip < count_chip - 1,
    )
    where = (
        {"line": line - 1}, {"line": line + 1},
        {"layer": layer - 1}, {"layer": layer + 1},
        {"chip": chip - 1}, {"chip": chip + 1},
    )
    sends = (line_send, line_send, layer_send, layer_send, chip_send, chip_send)
    recvs = (line_recv, line_recv, layer_recv, layer_recv, chip_recv, chip_recv)

    other = line + 1 - 2 * lax.rem(line, 2)
    offsets = [4, 2, count_line - 2]
    peers = [lax.rem(core + step, count_line) for step in offsets for core in (line, other)] + [other]
    sources = [peers[n] for n in (0, 1, 4, 5, 2, 3, 6)]

    barrier = pltpu.get_barrier_semaphore()
    for side in range(2, 6):
        @pl.when(has[side])
        def _():
            pl.semaphore_signal(barrier, inc=1, device_id=where[side], device_id_type=MESH)
    greets = [((line > 0) & (peer > 0)) | (line + peer == 1) for peer in peers]
    for n in (6, 2, 3, 4, 5, 0, 1):
        @pl.when(greets[n])
        def _():
            pl.semaphore_signal(barrier, inc=1, device_id={"line": peers[n]}, device_id_type=MESH)

    loads = [
        pltpu.make_async_copy(src, dst, in_sem.at[n])
        for n, (src, dst) in enumerate(
            (
                (label_hbm, label), (temp_hbm, temp), (lut_hbm, lut),
                (weight_hbm, weight), (power_hbm, power),
            )
        )
    ]
    for load in loads:
        load.start()

    for side in range(6):
        @pl.when(jnp.logical_not(has[side]))
        def _():
            recvs[side][side % 2] = jnp.zeros(recvs[side].shape[1:], F32)

    def halo(side):
        return pltpu.make_async_remote_copy(
            src_ref=sends[side] if side >= 4 else sends[side].at[side % 2],
            dst_ref=recvs[side].at[1 - side % 2],
            send_sem=halo_send_sem.at[side],
            recv_sem=halo_recv_sem.at[side - side % 2 + 1 - side % 2],
            device_id=where[side],
            device_id_type=MESH,
        )

    def halo_start(side):
        @pl.when(has[side])
        def _():
            halo(side).start()

    def halo_landed(side):
        @pl.when(has[side])
        def _():
            pltpu.make_async_remote_copy(
                src_ref=sends[side] if side >= 4 else sends[side].at[side % 2],
                dst_ref=recvs[side].at[side % 2],
                send_sem=halo_send_sem.at[side],
                recv_sem=halo_recv_sem.at[side],
                device_id=where[side],
                device_id_type=MESH,
            ).wait_recv()

    loads[0].wait()
    loads[1].wait()
    start, stop = spot(0, 0), spot(RUNS - 1, STEPS - 1)
    for end, face in ((0, start), (1, stop)):
        line_send[end, 0] = temp[face, :]
        line_send[end, 1] = label[face, :].astype(F32)
    for end, first in ((0, 0), (1, depth - 1)):
        face = pl.ds(first, rows, stride=depth)
        layer_send[end, 0] = temp[face, :]
        layer_send[end, 1] = label[face, :].astype(F32)

    lane = lax.broadcasted_iota(jnp.int32, (1, 1, width), 2)
    packed = jnp.zeros((RUNS, depth, width), F32)
    for i in range(STEPS):
        packed = jnp.where(
            lane // 2 == 2 * i, pltpu.roll(read(temp, i), 4 * i + 1, 2),
            jnp.where(
                lane // 2 == 2 * i + 1,
                pltpu.roll(read(label, i).astype(F32), 4 * i + 3, 2),
                packed,
            ),
        )
    packed = packed.reshape(2, 4, depth, width)
    dense = packed[:, 0]
    for k in range(1, 4):
        dense = jnp.where(lane // 32 == k, pltpu.roll(packed[:, k], 32 * k, 2), dense)
    chip_send[...] = dense

    pl.semaphore_wait(barrier, sum(met.astype(jnp.int32) for met in greets + list(has[2:])))
    for side in (4, 5, 2, 3, 0, 1):
        halo_start(side)

    @pl.when(line == 1)
    def _():
        for peer in [peers[n] for n in (6, 0, 1, 2, 3, 4, 5)]:
            pl.semaphore_signal(ready_sem, inc=1, device_id={"line": peer}, device_id_type=MESH)

    loads[2].wait()
    values = [lut[n] for n in range(8)]

    def look_up(tags):
        odd = (tags & 1) == 1
        two = (tags & 2) == 2
        four = tags >= 4
        pairs = [jnp.where(odd, values[2 * n + 1], values[2 * n]) for n in range(4)]
        halves = [jnp.where(two, pairs[2 * n + 1], pairs[2 * n]) for n in range(2)]
        return jnp.where(four, halves[1], halves[0])

    def face_look_up(tags):
        return look_up(tags.astype(jnp.int32))

    for i in range(STEPS):
        write(cond, i, look_up(read(label, i)))

    for i in range(STEPS - 1):
        gx[:, i] = conductance(read(cond, i), read(cond, i + 1))
    k_last, k_first = read(cond, STEPS - 1), read(cond, 0)
    join = conductance(k_last, jnp.concatenate([k_first[1:], k_first[:1]], axis=0))
    gx[:, STEPS - 1] = join

    loads[3].wait()
    ya, c, yb = weight[:, 0], gx[:, 0], weight[:, 1]
    for i in range(1, STEPS - 1):
        u, t, inv = eliminate(c, yb, gx[:, i])
        ya = ya + u * yb
        c = c * t
        yb = weight[:, i + 1] + t * yb
        coef_u[:, i] = u
        coef_t[:, i] = t
        coef_q[:, i] = inv
    tree = []
    while ya.shape[0] > 1:
        half = ya.shape[0] // 2
        ya_l, ya_r = (ya.reshape(half, 2, depth, width)[:, n] for n in range(2))
        yb_l, yb_r = (yb.reshape(half, 2, depth, width)[:, n] for n in range(2))
        c_l, c_r = (c.reshape(half, 2, depth, width)[:, n] for n in range(2))
        g, join = (join.reshape(half, 2, depth, width)[:, n] for n in range(2))
        first = eliminate(c_l, yb_l, g)
        u, t, _ = first
        ya = ya_l + u * yb_l
        c = c_l * t
        mid = ya_r + t * yb_l
        second = eliminate(c, mid, c_r)
        u, t, _ = second
        ya = ya + u * mid
        c = c * t
        yb = yb_r + t * mid
        tree.append((first, second))
    ya, c, yb = ya[0], c[0], yb[0]
    t_a, u_a, inv_a = eliminate(2.0 * k_first[0], ya, c)
    y_left, yb, c = t_a * ya, yb + u_a * ya, t_a * c
    u_b, t_b, inv_b = eliminate(c, yb, 2.0 * k_last[RUNS - 1])
    y_left, y_right, c = y_left + u_b * yb, t_b * yb, c * t_b
    mats[line, 0] = y_left
    mats[line, 1] = c
    mats[line, 2] = y_right

    def spread(block, send_sem, recv_sem):
        return [
            pltpu.make_async_remote_copy(
                src_ref=block.at[line],
                dst_ref=block.at[line],
                send_sem=send_sem.at[n],
                recv_sem=recv_sem.at[n],
                device_id={"line": peer},
                device_id_type=MESH,
            )
            for n, peer in enumerate(peers)
        ]

    def landed(block, send_sem, recv_sem):
        for n, source in enumerate(sources):
            pltpu.make_async_remote_copy(
                src_ref=block.at[source],
                dst_ref=block.at[source],
                send_sem=send_sem.at[n],
                recv_sem=recv_sem.at[n],
                device_id={"line": source},
                device_id_type=MESH,
            ).wait_recv()

    mat_copies = spread(mats, mat_send_sem, mat_recv_sem)

    @pl.when(line == 0)
    def _():
        pl.semaphore_wait(ready_sem, 1)

    def start_others(copies):
        for peer, copy in zip(peers, copies):
            @pl.when(peer > 0)
            def _():
                copy.start()

    def start_first(copies):
        for peer, copy in zip(peers, copies):
            @pl.when(peer == 0)
            def _():
                copy.start()

    start_others(mat_copies)

    loads[4].wait()
    row = lax.broadcasted_iota(jnp.int32, (1, depth, 1), 1)
    flow = None
    for i in range(STEPS):
        heat_here, k_here = read(temp, i), read(cond, i)
        flow_y = jnp.where(
            lane == width - 1, 0.0,
            conductance(k_here, pltpu.roll(k_here, width - 1, 2))
            * (heat_here - pltpu.roll(heat_here, width - 1, 2)),
        )
        flow_z = jnp.where(
            row == depth - 1, 0.0,
            conductance(k_here, pltpu.roll(k_here, depth - 1, 1))
            * (heat_here - pltpu.roll(heat_here, depth - 1, 1)),
        )
        part = (
            power[:, i]
            - (flow_y - pltpu.roll(flow_y, 1, 2))
            - (flow_z - pltpu.roll(flow_z, 1, 1))
        )
        if i < STEPS - 1:
            flow_on = gx[:, i] * (heat_here - read(temp, i + 1))
        else:
            flow_on = gx[:-1, i] * (heat_here[:-1] - read(temp, 0)[1:])
            flow_on = jnp.concatenate([flow_on, jnp.zeros((1, depth, width), F32)], axis=0)
        if i > 0:
            part = part + flow
        write(res, i, part - flow_on)
        flow = flow_on
    for run in range(1, RUNS):
        here = spot(run, 0)
        res[here, :] = res[here, :] + flow[run - 1]

    halo_landed(0)
    halo_landed(1)
    for end, face in ((0, start), (1, stop)):
        g = conductance(cond[face, :], face_look_up(line_recv[end, 1]))
        g = jnp.where(has[end], g, 0.0)
        res[face, :] = res[face, :] - g * (temp[face, :] - line_recv[end, 0])
    halo_landed(2)
    halo_landed(3)
    is_top = layer == count_layer - 1
    for end, first in ((0, 0), (1, depth - 1)):
        face = pl.ds(first, rows, stride=depth)
        own_k = cond[face, :]
        g = conductance(own_k, face_look_up(layer_recv[end, 1]))
        if end == 0:
            g = jnp.where(has[2], g, 0.0)
        else:
            g = jnp.where(is_top, own_k, g)
        res[face, :] = res[face, :] - g * (layer_send[end, 0] - layer_recv[end, 0])

    own = chip_send[...]
    own_k = face_look_up(pltpu.roll(own, width - 2, 2))
    halo_landed(4)
    halo_landed(5)
    beside = jnp.where(
        lane % 2 == 0, pltpu.roll(chip_recv[1], width - 1, 2), pltpu.roll(chip_recv[0], 1, 2)
    )
    beside_k = face_look_up(pltpu.roll(beside, width - 2, 2))
    open_lane = ((lane % 4 == 0) & has[5]) | ((lane % 4 == 1) & has[4])
    edge = jnp.where(open_lane, conductance(own_k, beside_k) * (own - beside), 0.0)
    edges = jnp.stack(
        [edge] + [pltpu.roll(edge, width - 32 * k, 2) for k in range(1, 4)], axis=1
    ).reshape(RUNS, depth, width)
    at_edge = (lane == 0) | (lane == width - 1)
    for i in range(STEPS):
        total_res = read(res, i) - jnp.where(
            at_edge, pltpu.roll(edges, width - 1 - 4 * i, 2), 0.0
        )
        write(res, i, total_res)
        right = total_res.astype(jnp.bfloat16).astype(F32)
        if i == 0:
            ra = right
        elif i == 1:
            rb = right
        else:
            ra = ra + coef_u[:, i - 1] * rb
            held = coef_t[:, i - 1] * rb
            coef_q[:, i - 1] = coef_q[:, i - 1] * rb
            rb = right + held

    held = []
    for (u1, t1, inv1), (u2, t2, inv2) in tree:
        half = ra.shape[0] // 2
        ra_l, ra_r = (ra.reshape(half, 2, depth, width)[:, n] for n in range(2))
        rb_l, rb_r = (rb.reshape(half, 2, depth, width)[:, n] for n in range(2))
        mid = ra_r + t1 * rb_l
        held.append((inv1 * rb_l, inv2 * mid))
        ra = ra_l + u1 * rb_l + u2 * mid
        rb = rb_r + t2 * mid
    ra, rb = ra[0], rb[0]
    rb = rb + u_a * ra
    r_left, r_right = t_a * ra + u_b * rb, t_b * rb
    rights[line, 0] = r_left
    rights[line, 1] = r_right
    rhs_copies = spread(rights, rhs_send_sem, rhs_recv_sem)
    start_others(rhs_copies)

    @pl.when(line > 1)
    def _():
        pl.semaphore_wait(ready_sem, 1)

    start_first(mat_copies)
    start_first(rhs_copies)
    q_a, q_b = inv_a * ra, inv_b * rb

    landed(mats, mat_send_sem, mat_recv_sem)
    zero = jnp.zeros((depth, width), F32)
    before, after = zero, zero
    up, down = [], []
    for j in range(count_line - 1):
        a = before + mats[j, 0]
        u = mats[j, 1] * recip(a + mats[j, 1])
        before = jnp.where(j < line, mats[j, 2] + u * a, before)
        up.append(u)
        n = count_line - 1 - j
        a = after + mats[n, 2]
        u = mats[n, 1] * recip(a + mats[n, 1])
        after = jnp.where(n > line, mats[n, 0] + u * a, after)
        down.append(u)
    a = y_left + before
    b = y_right + after
    inv = recip(a * b + c * (a + b))
    from_a, from_b, cross = (b + c) * inv, (a + c) * inv, c * inv

    landed(rights, rhs_send_sem, rhs_recv_sem)
    left_in, right_in = zero, zero
    for j in range(count_line - 1):
        new = rights[j, 1] + up[j] * (rights[j, 0] + left_in)
        left_in = jnp.where(j < line, new, left_in)
        n = count_line - 1 - j
        new = rights[n, 0] + down[j] * (rights[n, 1] + right_in)
        right_in = jnp.where(n > line, new, right_in)
    left_in = left_in + r_left
    right_in = right_in + r_right
    x_left = from_a * left_in + cross * right_in
    x_right = cross * left_in + from_b * right_in
    xb = q_b + u_b * x_left + t_b * x_right
    xa = q_a + t_a * x_left + u_a * xb
    xa, xb = xa[None], xb[None]

    for ((u1, t1, _), (u2, t2, _)), (q1, q2) in zip(reversed(tree), reversed(held)):
        xr = q2 + u2 * xa + t2 * xb
        xl = q1 + u1 * xa + t1 * xr
        size = 2 * xa.shape[0]
        xa = jnp.stack([xa, xr], axis=1).reshape(size, depth, width)
        xb = jnp.stack([xl, xb], axis=1).reshape(size, depth, width)
    heat[:, 0] = weight[:, 0] * xa
    heat[:, STEPS - 1] = weight[:, STEPS - 1] * xb
    x = xb
    for i in range(STEPS - 2, 0, -1):
        x = coef_q[:, i] + coef_u[:, i] * xa + coef_t[:, i] * x
        heat[:, i] = weight[:, i] * x

    for side in range(6):
        @pl.when(has[side])
        def _():
            halo(side).wait_send()
    for copy in mat_copies + rhs_copies:
        copy.wait_send()


def store(res, heat, res_hbm, heat_hbm, sem):
    copies = [
        pltpu.make_async_copy(res, res_hbm, sem.at[0]),
        pltpu.make_async_copy(heat, heat_hbm, sem.at[1]),
    ]
    for copy in copies:
        copy.start()
    for copy in copies:
        copy.wait()


def shards(counts, warmth_field, power_input, inertia_weight, conductivity_lookup, substance_label):
    depth, width = warmth_field.shape[1:]
    shape = (RUNS, STEPS, depth, width)
    vmem = pltpu.VMEM
    whole = vmem(shape, F32)
    others = counts[0] - 1
    dma = pltpu.SemaphoreType.DMA
    hbm_space = pl.BlockSpec(memory_space=pltpu.HBM)
    vmem_space = pl.BlockSpec(memory_space=pltpu.VMEM)
    flat = (RUNS * STEPS * depth, width)
    rows = vmem(flat, F32)
    residual, heat_rate = pl.pallas_call(
        functools.partial(kernel, *counts),
        out_shape=(rows, whole),
        in_specs=[hbm_space] * 5,
        out_specs=(vmem_space, vmem_space),
        scratch_shapes=[
            rows, whole, whole, vmem(flat, jnp.int32), pltpu.SMEM((8,), F32), rows,
            whole, whole, whole, whole,
            vmem((2, 2, depth, width), F32), vmem((2, 2, depth, width), F32),
            vmem((2, 2, RUNS * STEPS, width), F32), vmem((2, 2, RUNS * STEPS, width), F32),
            vmem((2, depth, width), F32), vmem((2, 2, depth, width), F32),
            vmem((counts[0], 3, depth, width), F32), vmem((counts[0], 2, depth, width), F32),
            dma((5,)), dma((6,)), dma((6,)),
            dma((others,)), dma((others,)), dma((others,)), dma((others,)),
            pltpu.SemaphoreType.REGULAR,
        ],
        compiler_params=pltpu.CompilerParams(
            collective_id=0, has_side_effects=True, vmem_limit_bytes=32 * 1024 * 1024
        ),
    )(
        *(
            pltpu.with_memory_space_constraint(operand, pltpu.HBM)
            for operand in (
                warmth_field.reshape(flat), power_input.reshape(shape),
                inertia_weight.reshape(shape), conductivity_lookup,
                substance_label.reshape(flat),
            )
        )
    )
    residual, heat_rate = pl.pallas_call(
        store,
        out_shape=(jax.ShapeDtypeStruct(flat, F32), jax.ShapeDtypeStruct(shape, F32)),
        in_specs=[pl.BlockSpec(memory_space=pl.ANY)] * 2,
        out_specs=(hbm_space, hbm_space),
        scratch_shapes=[dma((2,))],
    )(
        pltpu.with_memory_space_constraint(residual, pltpu.VMEM),
        pltpu.with_memory_space_constraint(heat_rate, pltpu.VMEM),
    )
    return residual.reshape(warmth_field.shape), heat_rate.reshape(warmth_field.shape)


def solution(mesh):
    counts = tuple(mesh.shape[axis] for axis in ("line", "chip", "layer"))
    spec = P("line", "layer", "chip")
    return jax.shard_map(
        functools.partial(shards, counts),
        mesh=mesh,
        in_specs=(spec, spec, spec, P(), spec),
        out_specs=(spec, spec),
        check_vma=False,
    )
```

```python
import functools

import jax
import jax.numpy as jnp
from jax import lax
from jax.experimental import pallas as pl
from jax.experimental.pallas import tpu as pltpu
from jax.sharding import PartitionSpec as P

MESH = pl.DeviceIdType.MESH
RUNS = 8
STEPS = 8
F32 = jnp.float32


def recip(x):
    return pltpu.reciprocal(x, approx=True)


def conductance(first, second):
    return 2.0 * first * second * recip(first + second)


def eliminate(left, ground, right):
    inv = recip(left + ground + right)
    return left * inv, right * inv, inv


PAD = 8


def spot(run, step, shift=0):
    return pl.ds((run * STEPS + step) * 16 + shift, 16)


def read(ref, step, shift=0):
    return jnp.stack([ref[spot(run, step, shift), :] for run in range(RUNS)])


def write(ref, step, value, shift=0):
    for run in range(RUNS):
        ref[spot(run, step, shift), :] = value[run]


def kernel(
    count_line, count_chip, count_layer,
    temp_hbm, power_hbm, weight_hbm, lut_hbm, label_hbm,
    res, heat,
    temp, power, weight, label, lut, cond,
    gx, coef_t, coef_u, coef_q,
    line_send, line_recv, layer_send, layer_recv, chip_send, chip_recv,
    mats, rights,
    in_sem, halo_send_sem, halo_recv_sem,
    mat_send_sem, mat_recv_sem, rhs_send_sem, rhs_recv_sem, ready_sem,
):
    line = lax.axis_index("line")
    chip = lax.axis_index("chip")
    layer = lax.axis_index("layer")
    depth, width = 16, 128
    rows = RUNS * STEPS

    has = (
        line > 0, line < count_line - 1,
        layer > 0, layer < count_layer - 1,
        chip > 0, chip < count_chip - 1,
    )
    where = (
        {"line": line - 1}, {"line": line + 1},
        {"layer": layer - 1}, {"layer": layer + 1},
        {"chip": chip - 1}, {"chip": chip + 1},
    )
    sends = (line_send, line_send, layer_send, layer_send, chip_send, chip_send)
    recvs = (line_recv, line_recv, layer_recv, layer_recv, chip_recv, chip_recv)

    other = line + 1 - 2 * lax.rem(line, 2)
    offsets = [4, 2, count_line - 2]
    peers = [lax.rem(core + step, count_line) for step in offsets for core in (line, other)] + [other]
    sources = [peers[n] for n in (0, 1, 4, 5, 2, 3, 6)]

    barrier = pltpu.get_barrier_semaphore()
    for side in range(2, 6):
        @pl.when(has[side])
        def _():
            pl.semaphore_signal(barrier, inc=1, device_id=where[side], device_id_type=MESH)
    first_lines = (chip == 0) & (layer == 0)
    other_lines = jnp.logical_not(first_lines)
    greets = [other_lines | ((line > 0) & (peer > 0)) | (line + peer == 1) for peer in peers]
    for n in (6, 2, 3, 4, 5, 0, 1):
        @pl.when(greets[n])
        def _():
            pl.semaphore_signal(barrier, inc=1, device_id={"line": peers[n]}, device_id_type=MESH)

    loads = [
        pltpu.make_async_copy(src, dst, in_sem.at[n])
        for n, (src, dst) in enumerate(
            (
                (label_hbm, label), (temp_hbm, temp.at[pl.ds(PAD, rows * depth)]), (lut_hbm, lut),
                (weight_hbm, weight), (power_hbm, power),
            )
        )
    ]
    for load in loads:
        load.start()

    for side in range(6):
        @pl.when(jnp.logical_not(has[side]))
        def _():
            recvs[side][side % 2] = jnp.zeros(recvs[side].shape[1:], F32)

    def halo(side):
        return pltpu.make_async_remote_copy(
            src_ref=sends[side] if side >= 4 else sends[side].at[side % 2],
            dst_ref=recvs[side].at[1 - side % 2],
            send_sem=halo_send_sem.at[side],
            recv_sem=halo_recv_sem.at[side - side % 2 + 1 - side % 2],
            device_id=where[side],
            device_id_type=MESH,
        )

    def halo_start(side):
        @pl.when(has[side])
        def _():
            halo(side).start()

    def halo_landed(side):
        @pl.when(has[side])
        def _():
            pltpu.make_async_remote_copy(
                src_ref=sends[side] if side >= 4 else sends[side].at[side % 2],
                dst_ref=recvs[side].at[side % 2],
                send_sem=halo_send_sem.at[side],
                recv_sem=halo_recv_sem.at[side],
                device_id=where[side],
                device_id_type=MESH,
            ).wait_recv()

    for ref in (temp, cond):
        for first in (0, rows * depth + PAD):
            ref[pl.ds(first, PAD), :] = jnp.zeros((PAD, width), F32)

    loads[0].wait()
    loads[1].wait()
    x_ends = ((0, 0), (RUNS - 1, STEPS - 1))
    z_ends = (0, depth - 1)
    for end in range(2):
        line_send[end, 0] = temp[spot(*x_ends[end], PAD), :]
        line_send[end, 1] = label[spot(*x_ends[end]), :].astype(F32)
        layer_send[end, 0] = temp[pl.ds(z_ends[end] + PAD, rows, stride=depth), :]
        layer_send[end, 1] = label[pl.ds(z_ends[end], rows, stride=depth), :].astype(F32)

    lane = lax.broadcasted_iota(jnp.int32, (1, 1, width), 2)
    packed = jnp.zeros((RUNS, depth, width), F32)
    for i in range(STEPS):
        packed = jnp.where(
            lane // 2 == 2 * i, pltpu.roll(read(temp, i, PAD), 4 * i + 1, 2),
            jnp.where(
                lane // 2 == 2 * i + 1,
                pltpu.roll(read(label, i).astype(F32), 4 * i + 3, 2),
                packed,
            ),
        )
    packed = packed.reshape(2, 4, depth, width)
    dense = packed[:, 0]
    for k in range(1, 4):
        dense = jnp.where(lane // 32 == k, pltpu.roll(packed[:, k], 32 * k, 2), dense)
    chip_send[...] = dense

    pl.semaphore_wait(barrier, sum(met.astype(jnp.int32) for met in greets + list(has[2:])))
    for side in (2, 3, 4, 5, 0, 1):
        halo_start(side)


    @pl.when(first_lines & (line == 1))
    def _():
        for peer in [peers[n] for n in (6, 0, 1, 2, 3, 4, 5)]:
            pl.semaphore_signal(ready_sem, inc=1, device_id={"line": peer}, device_id_type=MESH)

    loads[2].wait()
    values = [lut[n] for n in range(8)]

    def look_up(tags):
        odd = (tags & 1) == 1
        two = (tags & 2) == 2
        four = tags >= 4
        pairs = [jnp.where(odd, values[2 * n + 1], values[2 * n]) for n in range(4)]
        halves = [jnp.where(two, pairs[2 * n + 1], pairs[2 * n]) for n in range(2)]
        return jnp.where(four, halves[1], halves[0])

    def face_look_up(tags):
        return look_up(tags.astype(jnp.int32))

    for i in range(STEPS):
        write(cond, i, look_up(read(label, i)), PAD)

    for i in range(STEPS - 1):
        gx[:, i] = conductance(read(cond, i, PAD), read(cond, i + 1, PAD))
    k_last, k_first = read(cond, STEPS - 1, PAD), read(cond, 0, PAD)
    join = conductance(k_last, jnp.concatenate([k_first[1:], k_first[:1]], axis=0))
    gx[:, STEPS - 1] = join

    loads[3].wait()
    ya, c, yb = weight[:, 0], gx[:, 0], weight[:, 1]
    for i in range(1, STEPS - 1):
        u, t, inv = eliminate(c, yb, gx[:, i])
        ya = ya + u * yb
        c = c * t
        yb = weight[:, i + 1] + t * yb
        coef_u[:, i] = u
        coef_t[:, i] = t
        coef_q[:, i] = inv
    tree = []
    while ya.shape[0] > 1:
        half = ya.shape[0] // 2
        ya_l, ya_r = (ya.reshape(half, 2, depth, width)[:, n] for n in range(2))
        yb_l, yb_r = (yb.reshape(half, 2, depth, width)[:, n] for n in range(2))
        c_l, c_r = (c.reshape(half, 2, depth, width)[:, n] for n in range(2))
        g, join = (join.reshape(half, 2, depth, width)[:, n] for n in range(2))
        first = eliminate(c_l, yb_l, g)
        u, t, _ = first
        ya = ya_l + u * yb_l
        c = c_l * t
        mid = ya_r + t * yb_l
        second = eliminate(c, mid, c_r)
        u, t, _ = second
        ya = ya + u * mid
        c = c * t
        yb = yb_r + t * mid
        tree.append((first, second))
    ya, c, yb = ya[0], c[0], yb[0]
    t_a, u_a, inv_a = eliminate(2.0 * k_first[0], ya, c)
    y_left, yb, c = t_a * ya, yb + u_a * ya, t_a * c
    u_b, t_b, inv_b = eliminate(c, yb, 2.0 * k_last[RUNS - 1])
    y_left, y_right, c = y_left + u_b * yb, t_b * yb, c * t_b
    mats[line, 0] = y_left
    mats[line, 1] = c
    mats[line, 2] = y_right

    def spread(block, send_sem, recv_sem):
        return [
            pltpu.make_async_remote_copy(
                src_ref=block.at[line],
                dst_ref=block.at[line],
                send_sem=send_sem.at[n],
                recv_sem=recv_sem.at[n],
                device_id={"line": peer},
                device_id_type=MESH,
            )
            for n, peer in enumerate(peers)
        ]

    def landed(block, send_sem, recv_sem):
        for n, source in enumerate(sources):
            pltpu.make_async_remote_copy(
                src_ref=block.at[source],
                dst_ref=block.at[source],
                send_sem=send_sem.at[n],
                recv_sem=recv_sem.at[n],
                device_id={"line": source},
                device_id_type=MESH,
            ).wait_recv()

    mat_copies = spread(mats, mat_send_sem, mat_recv_sem)

    @pl.when(first_lines & (line == 0))
    def _():
        pl.semaphore_wait(ready_sem, 1)

    def start_others(copies):
        for peer, copy in zip(peers, copies):
            @pl.when(other_lines | (peer > 0))
            def _():
                copy.start()

    def start_first(copies):
        for peer, copy in zip(peers, copies):
            @pl.when(first_lines & (peer == 0))
            def _():
                copy.start()

    start_others(mat_copies)

    loads[4].wait()
    row = lax.broadcasted_iota(jnp.int32, (1, depth, 1), 1)
    flow = None
    for i in range(STEPS):
        heat_here, k_here = read(temp, i, PAD), read(cond, i, PAD)
        flow_y = jnp.where(
            lane == width - 1, 0.0,
            conductance(k_here, pltpu.roll(k_here, width - 1, 2))
            * (heat_here - pltpu.roll(heat_here, width - 1, 2)),
        )
        flow_up = jnp.where(
            row == depth - 1, 0.0,
            conductance(k_here, read(cond, i, PAD + 1)) * (heat_here - read(temp, i, PAD + 1)),
        )
        part = power[:, i] - (flow_y - pltpu.roll(flow_y, 1, 2)) - (flow_up - pltpu.roll(flow_up, 1, 1))
        if i < STEPS - 1:
            flow_on = gx[:, i] * (heat_here - read(temp, i + 1, PAD))
        else:
            flow_on = gx[:-1, i] * (heat_here[:-1] - read(temp, 0, PAD)[1:])
            flow_on = jnp.concatenate([flow_on, jnp.zeros((1, depth, width), F32)], axis=0)
        if i > 0:
            part = part + flow
        write(res, i, part - flow_on)
        flow = flow_on
    for run in range(1, RUNS):
        here = spot(run, 0)
        res[here, :] = res[here, :] + flow[run - 1]

    halo_landed(0)
    halo_landed(1)
    for end in range(2):
        here = spot(*x_ends[end])
        g = conductance(cond[spot(*x_ends[end], PAD), :], face_look_up(line_recv[end, 1]))
        g = jnp.where(has[end], g, 0.0)
        res[here, :] = res[here, :] - g * (line_send[end, 0] - line_recv[end, 0])

    own = chip_send[...]
    own_k = face_look_up(pltpu.roll(own, width - 2, 2))
    halo_landed(4)
    halo_landed(5)
    beside = jnp.where(
        lane % 2 == 0, pltpu.roll(chip_recv[1], width - 1, 2), pltpu.roll(chip_recv[0], 1, 2)
    )
    beside_k = face_look_up(pltpu.roll(beside, width - 2, 2))
    open_lane = ((lane % 4 == 0) & has[5]) | ((lane % 4 == 1) & has[4])
    edge = jnp.where(open_lane, conductance(own_k, beside_k) * (own - beside), 0.0)
    edges = jnp.stack(
        [edge] + [pltpu.roll(edge, width - 32 * k, 2) for k in range(1, 4)], axis=1
    ).reshape(RUNS, depth, width)
    at_edge = (lane == 0) | (lane == width - 1)
    for i in range(STEPS):
        write(res, i, read(res, i) - jnp.where(
            at_edge, pltpu.roll(edges, width - 1 - 4 * i, 2), 0.0
        ))

    is_top = layer == count_layer - 1
    own_faces = [cond[pl.ds(first + PAD, rows, stride=depth), :] for first in z_ends]
    halo_landed(2)
    halo_landed(3)
    for end in range(2):
        face = pl.ds(z_ends[end], rows, stride=depth)
        own_k = own_faces[end]
        g = conductance(own_k, face_look_up(layer_recv[end, 1]))
        if end == 0:
            g = jnp.where(has[2], g, 0.0)
        else:
            g = jnp.where(is_top, own_k, g)
        res[face, :] = res[face, :] - g * (layer_send[end, 0] - layer_recv[end, 0])
    for i in range(STEPS):
        right = read(res, i).astype(jnp.bfloat16).astype(F32)
        if i == 0:
            ra = right
        elif i == 1:
            rb = right
        else:
            ra = ra + coef_u[:, i - 1] * rb
            held = coef_t[:, i - 1] * rb
            coef_q[:, i - 1] = coef_q[:, i - 1] * rb
            rb = right + held

    held = []
    for (u1, t1, inv1), (u2, t2, inv2) in tree:
        half = ra.shape[0] // 2
        ra_l, ra_r = (ra.reshape(half, 2, depth, width)[:, n] for n in range(2))
        rb_l, rb_r = (rb.reshape(half, 2, depth, width)[:, n] for n in range(2))
        mid = ra_r + t1 * rb_l
        held.append((inv1 * rb_l, inv2 * mid))
        ra = ra_l + u1 * rb_l + u2 * mid
        rb = rb_r + t2 * mid
    ra, rb = ra[0], rb[0]
    rb = rb + u_a * ra
    r_left, r_right = t_a * ra + u_b * rb, t_b * rb
    rights[line, 0] = r_left
    rights[line, 1] = r_right
    rhs_copies = spread(rights, rhs_send_sem, rhs_recv_sem)
    start_others(rhs_copies)

    @pl.when(first_lines & (line > 1))
    def _():
        pl.semaphore_wait(ready_sem, 1)

    start_first(mat_copies)
    start_first(rhs_copies)
    q_a, q_b = inv_a * ra, inv_b * rb

    landed(mats, mat_send_sem, mat_recv_sem)
    zero = jnp.zeros((depth, width), F32)
    before, after = zero, zero
    up, down = [], []
    for j in range(count_line - 1):
        a = before + mats[j, 0]
        u = mats[j, 1] * recip(a + mats[j, 1])
        before = jnp.where(j < line, mats[j, 2] + u * a, before)
        up.append(u)
        n = count_line - 1 - j
        a = after + mats[n, 2]
        u = mats[n, 1] * recip(a + mats[n, 1])
        after = jnp.where(n > line, mats[n, 0] + u * a, after)
        down.append(u)
    a = y_left + before
    b = y_right + after
    inv = recip(a * b + c * (a + b))
    from_a, from_b, cross = (b + c) * inv, (a + c) * inv, c * inv

    landed(rights, rhs_send_sem, rhs_recv_sem)
    left_in, right_in = zero, zero
    for j in range(count_line - 1):
        new = rights[j, 1] + up[j] * (rights[j, 0] + left_in)
        left_in = jnp.where(j < line, new, left_in)
        n = count_line - 1 - j
        new = rights[n, 0] + down[j] * (rights[n, 1] + right_in)
        right_in = jnp.where(n > line, new, right_in)
    left_in = left_in + r_left
    right_in = right_in + r_right
    x_left = from_a * left_in + cross * right_in
    x_right = cross * left_in + from_b * right_in
    xb = q_b + u_b * x_left + t_b * x_right
    xa = q_a + t_a * x_left + u_a * xb
    xa, xb = xa[None], xb[None]

    for ((u1, t1, _), (u2, t2, _)), (q1, q2) in zip(reversed(tree), reversed(held)):
        xr = q2 + u2 * xa + t2 * xb
        xl = q1 + u1 * xa + t1 * xr
        size = 2 * xa.shape[0]
        xa = jnp.stack([xa, xr], axis=1).reshape(size, depth, width)
        xb = jnp.stack([xl, xb], axis=1).reshape(size, depth, width)
    heat[:, 0] = weight[:, 0] * xa
    heat[:, STEPS - 1] = weight[:, STEPS - 1] * xb
    x = xb
    for i in range(STEPS - 2, 0, -1):
        x = coef_q[:, i] + coef_u[:, i] * xa + coef_t[:, i] * x
        heat[:, i] = weight[:, i] * x

    for side in range(6):
        @pl.when(has[side])
        def _():
            halo(side).wait_send()
    for copy in mat_copies + rhs_copies:
        copy.wait_send()


def store(res, heat, res_hbm, heat_hbm, sem):
    copies = [
        pltpu.make_async_copy(res, res_hbm, sem.at[0]),
        pltpu.make_async_copy(heat, heat_hbm, sem.at[1]),
    ]
    for copy in copies:
        copy.start()
    for copy in copies:
        copy.wait()


def shards(counts, warmth_field, power_input, inertia_weight, conductivity_lookup, substance_label):
    depth, width = warmth_field.shape[1:]
    shape = (RUNS, STEPS, depth, width)
    vmem = pltpu.VMEM
    whole = vmem(shape, F32)
    others = counts[0] - 1
    dma = pltpu.SemaphoreType.DMA
    hbm_space = pl.BlockSpec(memory_space=pltpu.HBM)
    vmem_space = pl.BlockSpec(memory_space=pltpu.VMEM)
    flat = (RUNS * STEPS * depth, width)
    rows = vmem(flat, F32)
    padded = vmem((flat[0] + 2 * PAD, width), F32)
    residual, heat_rate = pl.pallas_call(
        functools.partial(kernel, *counts),
        out_shape=(rows, whole),
        in_specs=[hbm_space] * 5,
        out_specs=(vmem_space, vmem_space),
        scratch_shapes=[
            padded, whole, whole, vmem(flat, jnp.int32), pltpu.SMEM((8,), F32), padded,
            whole, whole, whole, whole,
            vmem((2, 2, depth, width), F32), vmem((2, 2, depth, width), F32),
            vmem((2, 2, RUNS * STEPS, width), F32), vmem((2, 2, RUNS * STEPS, width), F32),
            vmem((2, depth, width), F32), vmem((2, 2, depth, width), F32),
            vmem((counts[0], 3, depth, width), F32), vmem((counts[0], 2, depth, width), F32),
            dma((5,)), dma((6,)), dma((6,)),
            dma((others,)), dma((others,)), dma((others,)), dma((others,)),
            pltpu.SemaphoreType.REGULAR,
        ],
        compiler_params=pltpu.CompilerParams(
            collective_id=0, has_side_effects=True, vmem_limit_bytes=32 * 1024 * 1024
        ),
    )(
        *(
            pltpu.with_memory_space_constraint(operand, pltpu.HBM)
            for operand in (
                warmth_field.reshape(flat), power_input.reshape(shape),
                inertia_weight.reshape(shape), conductivity_lookup,
                substance_label.reshape(flat),
            )
        )
    )
    residual, heat_rate = pl.pallas_call(
        store,
        out_shape=(jax.ShapeDtypeStruct(flat, F32), jax.ShapeDtypeStruct(shape, F32)),
        in_specs=[pl.BlockSpec(memory_space=pl.ANY)] * 2,
        out_specs=(hbm_space, hbm_space),
        scratch_shapes=[dma((2,))],
    )(
        pltpu.with_memory_space_constraint(residual, pltpu.VMEM),
        pltpu.with_memory_space_constraint(heat_rate, pltpu.VMEM),
    )
    return residual.reshape(warmth_field.shape), heat_rate.reshape(warmth_field.shape)


def solution(mesh):
    counts = tuple(mesh.shape[axis] for axis in ("line", "chip", "layer"))
    spec = P("line", "layer", "chip")
    return jax.shard_map(
        functools.partial(shards, counts),
        mesh=mesh,
        in_specs=(spec, spec, spec, P(), spec),
        out_specs=(spec, spec),
        check_vma=False,
    )
```

```python
import functools

import jax
import jax.numpy as jnp
from jax import lax
from jax.experimental import pallas as pl
from jax.experimental.pallas import tpu as pltpu
from jax.sharding import PartitionSpec as P

MESH = pl.DeviceIdType.MESH
RUNS = 8
STEPS = 8
F32 = jnp.float32


def recip(x):
    return pltpu.reciprocal(x, approx=True)


def conductance(first, second):
    return 2.0 * first * second * recip(first + second)


def eliminate(left, ground, right):
    inv = recip(left + ground + right)
    return left * inv, right * inv, inv


PAD = 8


def spot(run, step, shift=0):
    return pl.ds((run * STEPS + step) * 16 + shift, 16)


def read(ref, step, shift=0):
    return jnp.stack([ref[spot(run, step, shift), :] for run in range(RUNS)])


def write(ref, step, value, shift=0):
    for run in range(RUNS):
        ref[spot(run, step, shift), :] = value[run]


def kernel(
    count_line, count_chip, count_layer,
    temp_hbm, power_hbm, weight_hbm, lut_hbm, label_hbm,
    res, weight, coef_t, coef_u, coef_q, run_ends,
    temp, power, label, lut, cond, gx,
    line_send, line_recv, layer_send, layer_recv, chip_send, chip_recv,
    mats, rights,
    in_sem, halo_send_sem, halo_recv_sem,
    mat_send_sem, mat_recv_sem, rhs_send_sem, rhs_recv_sem, ready_sem,
):
    line = lax.axis_index("line")
    chip = lax.axis_index("chip")
    layer = lax.axis_index("layer")
    depth, width = 16, 128
    rows = RUNS * STEPS

    has = (
        line > 0, line < count_line - 1,
        layer > 0, layer < count_layer - 1,
        chip > 0, chip < count_chip - 1,
    )
    where = (
        {"line": line - 1}, {"line": line + 1},
        {"layer": layer - 1}, {"layer": layer + 1},
        {"chip": chip - 1}, {"chip": chip + 1},
    )
    sends = (line_send, line_send, layer_send, layer_send, chip_send, chip_send)
    recvs = (line_recv, line_recv, layer_recv, layer_recv, chip_recv, chip_recv)

    other = line + 1 - 2 * lax.rem(line, 2)
    offsets = [4, 2, count_line - 2]
    peers = [lax.rem(core + step, count_line) for step in offsets for core in (line, other)] + [other]
    sources = [peers[n] for n in (0, 1, 4, 5, 2, 3, 6)]

    barrier = pltpu.get_barrier_semaphore()
    for side in range(2, 6):
        @pl.when(has[side])
        def _():
            pl.semaphore_signal(barrier, inc=1, device_id=where[side], device_id_type=MESH)
    loads = [
        pltpu.make_async_copy(src, dst, in_sem.at[n])
        for n, (src, dst) in enumerate(
            (
                (label_hbm, label), (temp_hbm, temp.at[pl.ds(PAD, rows * depth)]), (lut_hbm, lut),
                (weight_hbm, weight), (power_hbm, power),
            )
        )
    ]
    for load in loads:
        load.start()

    first_lines = (chip == 0) & (layer == 0)
    other_lines = jnp.logical_not(first_lines)
    greets = [other_lines | ((line > 0) & (peer > 0)) | (line + peer == 1) for peer in peers]
    for n in (6, 2, 3, 4, 5, 0, 1):
        @pl.when(greets[n])
        def _():
            pl.semaphore_signal(barrier, inc=1, device_id={"line": peers[n]}, device_id_type=MESH)


    for side in range(6):
        @pl.when(jnp.logical_not(has[side]))
        def _():
            recvs[side][side % 2] = jnp.zeros(recvs[side].shape[1:], F32)

    def halo(side):
        return pltpu.make_async_remote_copy(
            src_ref=sends[side] if side >= 4 else sends[side].at[side % 2],
            dst_ref=recvs[side].at[1 - side % 2],
            send_sem=halo_send_sem.at[side],
            recv_sem=halo_recv_sem.at[side - side % 2 + 1 - side % 2],
            device_id=where[side],
            device_id_type=MESH,
        )

    def halo_start(side):
        @pl.when(has[side])
        def _():
            halo(side).start()

    def halo_landed(side):
        @pl.when(has[side])
        def _():
            pltpu.make_async_remote_copy(
                src_ref=sends[side] if side >= 4 else sends[side].at[side % 2],
                dst_ref=recvs[side].at[side % 2],
                send_sem=halo_send_sem.at[side],
                recv_sem=halo_recv_sem.at[side],
                device_id=where[side],
                device_id_type=MESH,
            ).wait_recv()

    for ref in (temp, cond):
        for first in (0, rows * depth + PAD):
            ref[pl.ds(first, PAD), :] = jnp.zeros((PAD, width), F32)

    loads[0].wait()
    loads[1].wait()
    x_ends = ((0, 0), (RUNS - 1, STEPS - 1))
    z_ends = (0, depth - 1)
    for end in range(2):
        line_send[end, 0] = temp[spot(*x_ends[end], PAD), :]
        line_send[end, 1] = label[spot(*x_ends[end]), :].astype(F32)
        layer_send[end, 0] = temp[pl.ds(z_ends[end] + PAD, rows, stride=depth), :]
        layer_send[end, 1] = label[pl.ds(z_ends[end], rows, stride=depth), :].astype(F32)

    lane = lax.broadcasted_iota(jnp.int32, (1, 1, width), 2)
    packed = jnp.zeros((RUNS, depth, width), F32)
    for i in range(STEPS):
        packed = jnp.where(
            lane // 2 == 2 * i, pltpu.roll(read(temp, i, PAD), 4 * i + 1, 2),
            jnp.where(
                lane // 2 == 2 * i + 1,
                pltpu.roll(read(label, i).astype(F32), 4 * i + 3, 2),
                packed,
            ),
        )
    packed = packed.reshape(2, 4, depth, width)
    dense = packed[:, 0]
    for k in range(1, 4):
        dense = jnp.where(lane // 32 == k, pltpu.roll(packed[:, k], 32 * k, 2), dense)
    chip_send[...] = dense

    pl.semaphore_wait(barrier, sum(met.astype(jnp.int32) for met in greets + list(has[2:])))
    for side in (2, 3, 4, 5, 0, 1):
        halo_start(side)


    @pl.when(first_lines & (line == 1))
    def _():
        for peer in [peers[n] for n in (6, 0, 1, 2, 3, 4, 5)]:
            pl.semaphore_signal(ready_sem, inc=1, device_id={"line": peer}, device_id_type=MESH)

    loads[2].wait()
    values = [lut[n] for n in range(8)]

    def look_up(tags):
        odd = (tags & 1) == 1
        two = (tags & 2) == 2
        four = tags >= 4
        pairs = [jnp.where(odd, values[2 * n + 1], values[2 * n]) for n in range(4)]
        halves = [jnp.where(two, pairs[2 * n + 1], pairs[2 * n]) for n in range(2)]
        return jnp.where(four, halves[1], halves[0])

    def face_look_up(tags):
        return look_up(tags.astype(jnp.int32))

    for i in range(STEPS):
        write(cond, i, look_up(read(label, i)), PAD)

    for i in range(STEPS - 1):
        gx[:, i] = conductance(read(cond, i, PAD), read(cond, i + 1, PAD))
    k_last, k_first = read(cond, STEPS - 1, PAD), read(cond, 0, PAD)
    join = conductance(k_last, jnp.concatenate([k_first[1:], k_first[:1]], axis=0))
    gx[:, STEPS - 1] = join

    loads[3].wait()
    ya, c, yb = weight[:, 0], gx[:, 0], weight[:, 1]
    for i in range(1, STEPS - 1):
        u, t, inv = eliminate(c, yb, gx[:, i])
        ya = ya + u * yb
        c = c * t
        yb = weight[:, i + 1] + t * yb
        coef_u[:, i] = u
        coef_t[:, i] = t
        coef_q[:, i] = inv
    tree = []
    while ya.shape[0] > 1:
        half = ya.shape[0] // 2
        ya_l, ya_r = (ya.reshape(half, 2, depth, width)[:, n] for n in range(2))
        yb_l, yb_r = (yb.reshape(half, 2, depth, width)[:, n] for n in range(2))
        c_l, c_r = (c.reshape(half, 2, depth, width)[:, n] for n in range(2))
        g, join = (join.reshape(half, 2, depth, width)[:, n] for n in range(2))
        first = eliminate(c_l, yb_l, g)
        u, t, _ = first
        ya = ya_l + u * yb_l
        c = c_l * t
        mid = ya_r + t * yb_l
        second = eliminate(c, mid, c_r)
        u, t, _ = second
        ya = ya + u * mid
        c = c * t
        yb = yb_r + t * mid
        tree.append((first, second))
    ya, c, yb = ya[0], c[0], yb[0]
    t_a, u_a, inv_a = eliminate(2.0 * k_first[0], ya, c)
    y_left, yb, c = t_a * ya, yb + u_a * ya, t_a * c
    u_b, t_b, inv_b = eliminate(c, yb, 2.0 * k_last[RUNS - 1])
    y_left, y_right, c = y_left + u_b * yb, t_b * yb, c * t_b
    mats[line, 0] = y_left
    mats[line, 1] = c
    mats[line, 2] = y_right

    def spread(block, send_sem, recv_sem):
        return [
            pltpu.make_async_remote_copy(
                src_ref=block.at[line],
                dst_ref=block.at[line],
                send_sem=send_sem.at[n],
                recv_sem=recv_sem.at[n],
                device_id={"line": peer},
                device_id_type=MESH,
            )
            for n, peer in enumerate(peers)
        ]

    def landed(block, send_sem, recv_sem):
        for n, source in enumerate(sources):
            pltpu.make_async_remote_copy(
                src_ref=block.at[source],
                dst_ref=block.at[source],
                send_sem=send_sem.at[n],
                recv_sem=recv_sem.at[n],
                device_id={"line": source},
                device_id_type=MESH,
            ).wait_recv()

    mat_copies = spread(mats, mat_send_sem, mat_recv_sem)

    @pl.when(first_lines & (line == 0))
    def _():
        pl.semaphore_wait(ready_sem, 1)

    def start_others(copies):
        @pl.when(other_lines | (line == 0))
        def _():
            for copy in copies:
                copy.start()

        @pl.when(first_lines & (line > 0))
        def _():
            for peer, copy in zip(peers, copies):
                @pl.when(peer > 0)
                def _():
                    copy.start()

    def start_first(block, send_sem, recv_sem):
        n = sum(jnp.where(peer == 0, n, 0) for n, peer in enumerate(peers))

        @pl.when(first_lines & (line > 0))
        def _():
            pltpu.make_async_remote_copy(
                src_ref=block.at[line],
                dst_ref=block.at[line],
                send_sem=send_sem.at[n],
                recv_sem=recv_sem.at[n],
                device_id={"line": 0},
                device_id_type=MESH,
            ).start()

    start_others(mat_copies)

    loads[4].wait()
    row = lax.broadcasted_iota(jnp.int32, (1, depth, 1), 1)
    flow = None
    for i in range(STEPS):
        heat_here, k_here = read(temp, i, PAD), read(cond, i, PAD)
        flow_y = jnp.where(
            lane == width - 1, 0.0,
            conductance(k_here, pltpu.roll(k_here, width - 1, 2))
            * (heat_here - pltpu.roll(heat_here, width - 1, 2)),
        )
        flow_up = jnp.where(
            row == depth - 1, 0.0,
            conductance(k_here, read(cond, i, PAD + 1)) * (heat_here - read(temp, i, PAD + 1)),
        )
        part = power[:, i] - (flow_y - pltpu.roll(flow_y, 1, 2)) - (flow_up - pltpu.roll(flow_up, 1, 1))
        if i < STEPS - 1:
            flow_on = gx[:, i] * (heat_here - read(temp, i + 1, PAD))
        else:
            flow_on = gx[:-1, i] * (heat_here[:-1] - read(temp, 0, PAD)[1:])
            flow_on = jnp.concatenate([flow_on, jnp.zeros((1, depth, width), F32)], axis=0)
        if i > 0:
            part = part + flow
        write(res, i, part - flow_on)
        flow = flow_on
    for run in range(1, RUNS):
        here = spot(run, 0)
        res[here, :] = res[here, :] + flow[run - 1]

    @pl.when(first_lines & (line > 1))
    def _():
        pl.semaphore_wait(ready_sem, 1)

    start_first(mats, mat_send_sem, mat_recv_sem)

    halo_landed(0)
    halo_landed(1)
    for end in range(2):
        here = spot(*x_ends[end])
        g = conductance(cond[spot(*x_ends[end], PAD), :], face_look_up(line_recv[end, 1]))
        g = jnp.where(has[end], g, 0.0)
        res[here, :] = res[here, :] - g * (line_send[end, 0] - line_recv[end, 0])

    own = chip_send[...]
    own_k = face_look_up(pltpu.roll(own, width - 2, 2))
    halo_landed(4)
    halo_landed(5)
    beside = jnp.where(
        lane % 2 == 0, pltpu.roll(chip_recv[1], width - 1, 2), pltpu.roll(chip_recv[0], 1, 2)
    )
    beside_k = face_look_up(pltpu.roll(beside, width - 2, 2))
    open_lane = ((lane % 4 == 0) & has[5]) | ((lane % 4 == 1) & has[4])
    edge = jnp.where(open_lane, conductance(own_k, beside_k) * (own - beside), 0.0)
    edges = jnp.stack(
        [edge] + [pltpu.roll(edge, width - 32 * k, 2) for k in range(1, 4)], axis=1
    ).reshape(RUNS, depth, width)
    at_edge = (lane == 0) | (lane == width - 1)
    for i in range(STEPS):
        write(res, i, read(res, i) - jnp.where(
            at_edge, pltpu.roll(edges, width - 1 - 4 * i, 2), 0.0
        ))

    is_top = layer == count_layer - 1
    own_faces = [cond[pl.ds(first + PAD, rows, stride=depth), :] for first in z_ends]
    halo_landed(2)
    halo_landed(3)
    for end in range(2):
        face = pl.ds(z_ends[end], rows, stride=depth)
        own_k = own_faces[end]
        g = conductance(own_k, face_look_up(layer_recv[end, 1]))
        if end == 0:
            g = jnp.where(has[2], g, 0.0)
        else:
            g = jnp.where(is_top, own_k, g)
        res[face, :] = res[face, :] - g * (layer_send[end, 0] - layer_recv[end, 0])
    for i in range(STEPS):
        right = read(res, i).astype(jnp.bfloat16).astype(F32)
        if i == 0:
            ra = right
        elif i == 1:
            rb = right
        else:
            ra = ra + coef_u[:, i - 1] * rb
            held = coef_t[:, i - 1] * rb
            coef_q[:, i - 1] = coef_q[:, i - 1] * rb
            rb = right + held

    held = []
    for (u1, t1, inv1), (u2, t2, inv2) in tree:
        half = ra.shape[0] // 2
        ra_l, ra_r = (ra.reshape(half, 2, depth, width)[:, n] for n in range(2))
        rb_l, rb_r = (rb.reshape(half, 2, depth, width)[:, n] for n in range(2))
        mid = ra_r + t1 * rb_l
        held.append((inv1 * rb_l, inv2 * mid))
        ra = ra_l + u1 * rb_l + u2 * mid
        rb = rb_r + t2 * mid
    ra, rb = ra[0], rb[0]
    rb = rb + u_a * ra
    r_left, r_right = t_a * ra + u_b * rb, t_b * rb
    rights[line, 0] = r_left
    rights[line, 1] = r_right
    rhs_copies = spread(rights, rhs_send_sem, rhs_recv_sem)
    start_others(rhs_copies)

    start_first(rights, rhs_send_sem, rhs_recv_sem)
    q_a, q_b = inv_a * ra, inv_b * rb

    landed(mats, mat_send_sem, mat_recv_sem)
    zero = jnp.zeros((depth, width), F32)
    before, after = zero, zero
    up, down = [], []
    for j in range(count_line - 1):
        a = before + mats[j, 0]
        u = mats[j, 1] * recip(a + mats[j, 1])
        before = jnp.where(j < line, mats[j, 2] + u * a, before)
        up.append(u)
        n = count_line - 1 - j
        a = after + mats[n, 2]
        u = mats[n, 1] * recip(a + mats[n, 1])
        after = jnp.where(n > line, mats[n, 0] + u * a, after)
        down.append(u)
    a = y_left + before
    b = y_right + after
    inv = recip(a * b + c * (a + b))
    from_a, from_b, cross = (b + c) * inv, (a + c) * inv, c * inv

    landed(rights, rhs_send_sem, rhs_recv_sem)
    left_in, right_in = zero, zero
    for j in range(count_line - 1):
        new = rights[j, 1] + up[j] * (rights[j, 0] + left_in)
        left_in = jnp.where(j < line, new, left_in)
        n = count_line - 1 - j
        new = rights[n, 0] + down[j] * (rights[n, 1] + right_in)
        right_in = jnp.where(n > line, new, right_in)
    left_in = left_in + r_left
    right_in = right_in + r_right
    x_left = from_a * left_in + cross * right_in
    x_right = cross * left_in + from_b * right_in
    xb = q_b + u_b * x_left + t_b * x_right
    xa = q_a + t_a * x_left + u_a * xb
    xa, xb = xa[None], xb[None]

    for ((u1, t1, _), (u2, t2, _)), (q1, q2) in zip(reversed(tree), reversed(held)):
        xr = q2 + u2 * xa + t2 * xb
        xl = q1 + u1 * xa + t1 * xr
        size = 2 * xa.shape[0]
        xa = jnp.stack([xa, xr], axis=1).reshape(size, depth, width)
        xb = jnp.stack([xl, xb], axis=1).reshape(size, depth, width)
    run_ends[0] = xa
    run_ends[1] = xb

    for side in range(6):
        @pl.when(has[side])
        def _():
            halo(side).wait_send()
    for copy in mat_copies + rhs_copies:
        copy.wait_send()


def finish(res, weight, coef_t, coef_u, coef_q, run_ends, res_hbm, heat_hbm, heat, sem):
    copies = [pltpu.make_async_copy(res, res_hbm, sem.at[2])]
    copies[0].start()
    xa, x = run_ends[0], run_ends[1]
    for i in range(STEPS - 1, -1, -1):
        if i == 0:
            x = xa
        elif i < STEPS - 1:
            x = coef_q[:, i] + coef_u[:, i] * xa + coef_t[:, i] * x
        heat[:, i] = weight[:, i] * x
        if i % 4 == 0:
            part = pl.ds(i, 4)
            copies.append(
                pltpu.make_async_copy(heat.at[:, part], heat_hbm.at[:, part], sem.at[i // 4])
            )
            copies[-1].start()
    for copy in copies:
        copy.wait()


def shards(counts, warmth_field, power_input, inertia_weight, conductivity_lookup, substance_label):
    depth, width = warmth_field.shape[1:]
    shape = (RUNS, STEPS, depth, width)
    vmem = pltpu.VMEM
    whole = vmem(shape, F32)
    others = counts[0] - 1
    dma = pltpu.SemaphoreType.DMA
    hbm_space = pl.BlockSpec(memory_space=pltpu.HBM)
    vmem_space = pl.BlockSpec(memory_space=pltpu.VMEM)
    flat = (RUNS * STEPS * depth, width)
    rows = vmem(flat, F32)
    padded = vmem((flat[0] + 2 * PAD, width), F32)
    held = pl.pallas_call(
        functools.partial(kernel, *counts),
        out_shape=(rows, whole, whole, whole, whole, vmem((2, RUNS, depth, width), F32)),
        in_specs=[hbm_space] * 5,
        out_specs=(vmem_space,) * 6,
        scratch_shapes=[
            padded, whole, vmem(flat, jnp.int32), pltpu.SMEM((8,), F32), padded, whole,
            vmem((2, 2, depth, width), F32), vmem((2, 2, depth, width), F32),
            vmem((2, 2, RUNS * STEPS, width), F32), vmem((2, 2, RUNS * STEPS, width), F32),
            vmem((2, depth, width), F32), vmem((2, 2, depth, width), F32),
            vmem((counts[0], 3, depth, width), F32), vmem((counts[0], 2, depth, width), F32),
            dma((5,)), dma((6,)), dma((6,)),
            dma((others,)), dma((others,)), dma((others,)), dma((others,)),
            pltpu.SemaphoreType.REGULAR,
        ],
        compiler_params=pltpu.CompilerParams(
            collective_id=0, has_side_effects=True, vmem_limit_bytes=32 * 1024 * 1024
        ),
    )(
        *(
            pltpu.with_memory_space_constraint(operand, pltpu.HBM)
            for operand in (
                warmth_field.reshape(flat), power_input.reshape(shape),
                inertia_weight.reshape(shape), conductivity_lookup,
                substance_label.reshape(flat),
            )
        )
    )
    residual, heat_rate = pl.pallas_call(
        finish,
        out_shape=(jax.ShapeDtypeStruct(flat, F32), jax.ShapeDtypeStruct(shape, F32)),
        in_specs=[vmem_space] * 6,
        out_specs=(hbm_space, hbm_space),
        scratch_shapes=[whole, dma((3,))],
    )(*(pltpu.with_memory_space_constraint(array, pltpu.VMEM) for array in held))
    return residual.reshape(warmth_field.shape), heat_rate.reshape(warmth_field.shape)


def solution(mesh):
    counts = tuple(mesh.shape[axis] for axis in ("line", "chip", "layer"))
    spec = P("line", "layer", "chip")
    return jax.shard_map(
        functools.partial(shards, counts),
        mesh=mesh,
        in_specs=(spec, spec, spec, P(), spec),
        out_specs=(spec, spec),
        check_vma=False,
    )
```

```python
import functools

import jax
import jax.numpy as jnp
from jax import lax
from jax.experimental import pallas as pl
from jax.experimental.pallas import tpu as pltpu
from jax.sharding import PartitionSpec as P

MESH = pl.DeviceIdType.MESH
RUNS = 8
STEPS = 8
F32 = jnp.float32


def recip(x):
    return pltpu.reciprocal(x, approx=True)


def conductance(first, second):
    return 2.0 * first * second * recip(first + second)


def eliminate(left, ground, right):
    inv = recip(left + ground + right)
    return left * inv, right * inv, inv


PAD = 8


def spot(run, step, shift=0):
    return pl.ds((run * STEPS + step) * 16 + shift, 16)


def read(ref, step, shift=0):
    return jnp.stack([ref[spot(run, step, shift), :] for run in range(RUNS)])


def write(ref, step, value, shift=0):
    for run in range(RUNS):
        ref[spot(run, step, shift), :] = value[run]


def kernel(
    count_line, count_chip, count_layer,
    temp_hbm, power_hbm, weight_hbm, lut_hbm, label_hbm,
    res, weight, coef_t, coef_u, coef_q, run_ends,
    temp, power, label, lut, cond, gx,
    line_send, line_recv, layer_send, layer_recv, chip_send, chip_recv,
    mats, rights,
    in_sem, halo_send_sem, halo_recv_sem,
    mat_send_sem, mat_recv_sem, rhs_send_sem, rhs_recv_sem, ready_sem,
):
    line = lax.axis_index("line")
    chip = lax.axis_index("chip")
    layer = lax.axis_index("layer")
    depth, width = 16, 128
    rows = RUNS * STEPS

    has = (
        line > 0, line < count_line - 1,
        layer > 0, layer < count_layer - 1,
        chip > 0, chip < count_chip - 1,
    )
    where = (
        {"line": line - 1}, {"line": line + 1},
        {"layer": layer - 1}, {"layer": layer + 1},
        {"chip": chip - 1}, {"chip": chip + 1},
    )
    sends = (line_send, line_send, layer_send, layer_send, chip_send, chip_send)
    recvs = (line_recv, line_recv, layer_recv, layer_recv, chip_recv, chip_recv)

    other = line + 1 - 2 * lax.rem(line, 2)
    offsets = [4, 2, count_line - 2]
    peers = [lax.rem(core + step, count_line) for step in offsets for core in (line, other)] + [other]
    sources = [peers[n] for n in (0, 1, 4, 5, 2, 3, 6)]

    barrier = pltpu.get_barrier_semaphore()
    for side in range(2, 6):
        @pl.when(has[side])
        def _():
            pl.semaphore_signal(barrier, inc=1, device_id=where[side], device_id_type=MESH)
    loads = [
        pltpu.make_async_copy(src, dst, in_sem.at[n])
        for n, (src, dst) in enumerate(
            (
                (label_hbm, label), (temp_hbm, temp.at[pl.ds(PAD, rows * depth)]), (lut_hbm, lut),
                (weight_hbm, weight), (power_hbm, power),
            )
        )
    ]
    for load in loads:
        load.start()

    first_lines = (chip == 0) & (layer == 0)
    other_lines = jnp.logical_not(first_lines)
    greets = [other_lines | ((line > 0) & (peer > 0)) | (line + peer == 1) for peer in peers]
    for n in (6, 2, 3, 4, 5, 0, 1):
        @pl.when(greets[n])
        def _():
            pl.semaphore_signal(barrier, inc=1, device_id={"line": peers[n]}, device_id_type=MESH)


    for side in range(6):
        @pl.when(jnp.logical_not(has[side]))
        def _():
            recvs[side][side % 2] = jnp.zeros(recvs[side].shape[1:], F32)

    def halo(side):
        return pltpu.make_async_remote_copy(
            src_ref=sends[side] if side >= 4 else sends[side].at[side % 2],
            dst_ref=recvs[side].at[1 - side % 2],
            send_sem=halo_send_sem.at[side],
            recv_sem=halo_recv_sem.at[side - side % 2 + 1 - side % 2],
            device_id=where[side],
            device_id_type=MESH,
        )

    def halo_start(side):
        @pl.when(has[side])
        def _():
            halo(side).start()

    def halo_landed(side):
        @pl.when(has[side])
        def _():
            pltpu.make_async_remote_copy(
                src_ref=sends[side] if side >= 4 else sends[side].at[side % 2],
                dst_ref=recvs[side].at[side % 2],
                send_sem=halo_send_sem.at[side],
                recv_sem=halo_recv_sem.at[side],
                device_id=where[side],
                device_id_type=MESH,
            ).wait_recv()

    for ref in (temp, cond):
        for first in (0, rows * depth + PAD):
            ref[pl.ds(first, PAD), :] = jnp.zeros((PAD, width), F32)

    loads[0].wait()
    loads[1].wait()
    x_ends = ((0, 0), (RUNS - 1, STEPS - 1))
    z_ends = (0, depth - 1)
    for end in range(2):
        line_send[end, 0] = temp[spot(*x_ends[end], PAD), :]
        line_send[end, 1] = label[spot(*x_ends[end]), :].astype(F32)
        layer_send[end, 0] = temp[pl.ds(z_ends[end] + PAD, rows, stride=depth), :]
        layer_send[end, 1] = label[pl.ds(z_ends[end], rows, stride=depth), :].astype(F32)

    lane = lax.broadcasted_iota(jnp.int32, (1, 1, width), 2)
    packed = jnp.zeros((RUNS, depth, width), F32)
    for i in range(STEPS):
        packed = jnp.where(
            lane // 2 == 2 * i, pltpu.roll(read(temp, i, PAD), 4 * i + 1, 2),
            jnp.where(
                lane // 2 == 2 * i + 1,
                pltpu.roll(read(label, i).astype(F32), 4 * i + 3, 2),
                packed,
            ),
        )
    packed = packed.reshape(2, 4, depth, width)
    dense = packed[:, 0]
    for k in range(1, 4):
        dense = jnp.where(lane // 32 == k, pltpu.roll(packed[:, k], 32 * k, 2), dense)
    chip_send[...] = dense

    pl.semaphore_wait(barrier, sum(met.astype(jnp.int32) for met in greets + list(has[2:])))
    for side in (1, 0, 2, 3, 4, 5):
        halo_start(side)


    @pl.when(first_lines & (line == 1))
    def _():
        for peer in [peers[n] for n in (6, 0, 1, 2, 3, 4, 5)]:
            pl.semaphore_signal(ready_sem, inc=1, device_id={"line": peer}, device_id_type=MESH)

    loads[2].wait()
    values = [lut[n] for n in range(8)]

    def look_up(tags):
        odd = (tags & 1) == 1
        two = (tags & 2) == 2
        four = tags >= 4
        pairs = [jnp.where(odd, values[2 * n + 1], values[2 * n]) for n in range(4)]
        halves = [jnp.where(two, pairs[2 * n + 1], pairs[2 * n]) for n in range(2)]
        return jnp.where(four, halves[1], halves[0])

    def face_look_up(tags):
        return look_up(tags.astype(jnp.int32))

    for i in range(STEPS):
        write(cond, i, look_up(read(label, i)), PAD)

    for i in range(STEPS - 1):
        gx[:, i] = conductance(read(cond, i, PAD), read(cond, i + 1, PAD))
    k_last, k_first = read(cond, STEPS - 1, PAD), read(cond, 0, PAD)
    join = conductance(k_last, jnp.concatenate([k_first[1:], k_first[:1]], axis=0))
    gx[:, STEPS - 1] = join

    loads[3].wait()
    ya, c, yb = weight[:, 0], gx[:, 0], weight[:, 1]
    for i in range(1, STEPS - 1):
        u, t, inv = eliminate(c, yb, gx[:, i])
        ya = ya + u * yb
        c = c * t
        yb = weight[:, i + 1] + t * yb
        coef_u[:, i] = u
        coef_t[:, i] = t
        coef_q[:, i] = inv
    tree = []
    while ya.shape[0] > 1:
        half = ya.shape[0] // 2
        ya_l, ya_r = (ya.reshape(half, 2, depth, width)[:, n] for n in range(2))
        yb_l, yb_r = (yb.reshape(half, 2, depth, width)[:, n] for n in range(2))
        c_l, c_r = (c.reshape(half, 2, depth, width)[:, n] for n in range(2))
        g, join = (join.reshape(half, 2, depth, width)[:, n] for n in range(2))
        first = eliminate(c_l, yb_l, g)
        u, t, _ = first
        ya = ya_l + u * yb_l
        c = c_l * t
        mid = ya_r + t * yb_l
        second = eliminate(c, mid, c_r)
        u, t, _ = second
        ya = ya + u * mid
        c = c * t
        yb = yb_r + t * mid
        tree.append((first, second))
    ya, c, yb = ya[0], c[0], yb[0]
    t_a, u_a, inv_a = eliminate(2.0 * k_first[0], ya, c)
    y_left, yb, c = t_a * ya, yb + u_a * ya, t_a * c
    u_b, t_b, inv_b = eliminate(c, yb, 2.0 * k_last[RUNS - 1])
    y_left, y_right, c = y_left + u_b * yb, t_b * yb, c * t_b
    mats[line, 0] = y_left
    mats[line, 1] = c
    mats[line, 2] = y_right

    def spread(block, send_sem, recv_sem):
        return [
            pltpu.make_async_remote_copy(
                src_ref=block.at[line],
                dst_ref=block.at[line],
                send_sem=send_sem.at[n],
                recv_sem=recv_sem.at[n],
                device_id={"line": peer},
                device_id_type=MESH,
            )
            for n, peer in enumerate(peers)
        ]

    def landed(block, send_sem, recv_sem):
        for n, source in enumerate(sources):
            pltpu.make_async_remote_copy(
                src_ref=block.at[source],
                dst_ref=block.at[source],
                send_sem=send_sem.at[n],
                recv_sem=recv_sem.at[n],
                device_id={"line": source},
                device_id_type=MESH,
            ).wait_recv()

    mat_copies = spread(mats, mat_send_sem, mat_recv_sem)

    @pl.when(first_lines & (line == 0))
    def _():
        pl.semaphore_wait(ready_sem, 1)

    def start_others(copies):
        @pl.when(other_lines | (line == 0))
        def _():
            for copy in copies:
                copy.start()

        @pl.when(first_lines & (line > 0))
        def _():
            for peer, copy in zip(peers, copies):
                @pl.when(peer > 0)
                def _():
                    copy.start()

    def start_first(block, send_sem, recv_sem):
        n = sum(jnp.where(peer == 0, n, 0) for n, peer in enumerate(peers))

        @pl.when(first_lines & (line > 0))
        def _():
            pltpu.make_async_remote_copy(
                src_ref=block.at[line],
                dst_ref=block.at[line],
                send_sem=send_sem.at[n],
                recv_sem=recv_sem.at[n],
                device_id={"line": 0},
                device_id_type=MESH,
            ).start()

    start_others(mat_copies)

    loads[4].wait()
    row = lax.broadcasted_iota(jnp.int32, (1, depth, 1), 1)
    flow = None
    for i in range(STEPS):
        heat_here, k_here = read(temp, i, PAD), read(cond, i, PAD)
        flow_y = jnp.where(
            lane == width - 1, 0.0,
            conductance(k_here, pltpu.roll(k_here, width - 1, 2))
            * (heat_here - pltpu.roll(heat_here, width - 1, 2)),
        )
        flow_up = jnp.where(
            row == depth - 1, 0.0,
            conductance(k_here, read(cond, i, PAD + 1)) * (heat_here - read(temp, i, PAD + 1)),
        )
        part = power[:, i] - (flow_y - pltpu.roll(flow_y, 1, 2)) - (flow_up - pltpu.roll(flow_up, 1, 1))
        if i < STEPS - 1:
            flow_on = gx[:, i] * (heat_here - read(temp, i + 1, PAD))
        else:
            flow_on = gx[:-1, i] * (heat_here[:-1] - read(temp, 0, PAD)[1:])
            flow_on = jnp.concatenate([flow_on, jnp.zeros((1, depth, width), F32)], axis=0)
        if i > 0:
            part = part + flow
        write(res, i, part - flow_on)
        flow = flow_on
    for run in range(1, RUNS):
        here = spot(run, 0)
        res[here, :] = res[here, :] + flow[run - 1]

    @pl.when(first_lines & (line > 1))
    def _():
        pl.semaphore_wait(ready_sem, 1)

    start_first(mats, mat_send_sem, mat_recv_sem)

    halo_landed(0)
    halo_landed(1)
    for end in range(2):
        here = spot(*x_ends[end])
        g = conductance(cond[spot(*x_ends[end], PAD), :], face_look_up(line_recv[end, 1]))
        g = jnp.where(has[end], g, 0.0)
        res[here, :] = res[here, :] - g * (line_send[end, 0] - line_recv[end, 0])

    own = chip_send[...]
    own_k = face_look_up(pltpu.roll(own, width - 2, 2))
    halo_landed(4)
    halo_landed(5)
    beside = jnp.where(
        lane % 2 == 0, pltpu.roll(chip_recv[1], width - 1, 2), pltpu.roll(chip_recv[0], 1, 2)
    )
    beside_k = face_look_up(pltpu.roll(beside, width - 2, 2))
    open_lane = ((lane % 4 == 0) & has[5]) | ((lane % 4 == 1) & has[4])
    edge = jnp.where(open_lane, conductance(own_k, beside_k) * (own - beside), 0.0)
    edges = jnp.stack(
        [edge] + [pltpu.roll(edge, width - 32 * k, 2) for k in range(1, 4)], axis=1
    ).reshape(RUNS, depth, width)
    at_edge = (lane == 0) | (lane == width - 1)
    for i in range(STEPS):
        write(res, i, read(res, i) - jnp.where(
            at_edge, pltpu.roll(edges, width - 1 - 4 * i, 2), 0.0
        ))

    is_top = layer == count_layer - 1
    own_faces = [cond[pl.ds(first + PAD, rows, stride=depth), :] for first in z_ends]
    halo_landed(2)
    halo_landed(3)
    for end in range(2):
        face = pl.ds(z_ends[end], rows, stride=depth)
        own_k = own_faces[end]
        g = conductance(own_k, face_look_up(layer_recv[end, 1]))
        if end == 0:
            g = jnp.where(has[2], g, 0.0)
        else:
            g = jnp.where(is_top, own_k, g)
        res[face, :] = res[face, :] - g * (layer_send[end, 0] - layer_recv[end, 0])
    for i in range(STEPS):
        right = read(res, i).astype(jnp.bfloat16).astype(F32)
        if i == 0:
            ra = right
        elif i == 1:
            rb = right
        else:
            ra = ra + coef_u[:, i - 1] * rb
            held = coef_t[:, i - 1] * rb
            coef_q[:, i - 1] = coef_q[:, i - 1] * rb
            rb = right + held

    held = []
    for (u1, t1, inv1), (u2, t2, inv2) in tree:
        half = ra.shape[0] // 2
        ra_l, ra_r = (ra.reshape(half, 2, depth, width)[:, n] for n in range(2))
        rb_l, rb_r = (rb.reshape(half, 2, depth, width)[:, n] for n in range(2))
        mid = ra_r + t1 * rb_l
        held.append((inv1 * rb_l, inv2 * mid))
        ra = ra_l + u1 * rb_l + u2 * mid
        rb = rb_r + t2 * mid
    ra, rb = ra[0], rb[0]
    rb = rb + u_a * ra
    r_left, r_right = t_a * ra + u_b * rb, t_b * rb
    rights[line, 0] = r_left
    rights[line, 1] = r_right
    rhs_copies = spread(rights, rhs_send_sem, rhs_recv_sem)
    start_others(rhs_copies)

    start_first(rights, rhs_send_sem, rhs_recv_sem)
    q_a, q_b = inv_a * ra, inv_b * rb

    landed(mats, mat_send_sem, mat_recv_sem)
    zero = jnp.zeros((depth, width), F32)
    before, after = zero, zero
    up, down = [], []
    for j in range(count_line - 1):
        a = before + mats[j, 0]
        u = mats[j, 1] * recip(a + mats[j, 1])
        before = jnp.where(j < line, mats[j, 2] + u * a, before)
        up.append(u)
        n = count_line - 1 - j
        a = after + mats[n, 2]
        u = mats[n, 1] * recip(a + mats[n, 1])
        after = jnp.where(n > line, mats[n, 0] + u * a, after)
        down.append(u)
    a = y_left + before
    b = y_right + after
    inv = recip(a * b + c * (a + b))
    from_a, from_b, cross = (b + c) * inv, (a + c) * inv, c * inv

    landed(rights, rhs_send_sem, rhs_recv_sem)
    left_in, right_in = zero, zero
    for j in range(count_line - 1):
        new = rights[j, 1] + up[j] * (rights[j, 0] + left_in)
        left_in = jnp.where(j < line, new, left_in)
        n = count_line - 1 - j
        new = rights[n, 0] + down[j] * (rights[n, 1] + right_in)
        right_in = jnp.where(n > line, new, right_in)
    left_in = left_in + r_left
    right_in = right_in + r_right
    x_left = from_a * left_in + cross * right_in
    x_right = cross * left_in + from_b * right_in
    xb = q_b + u_b * x_left + t_b * x_right
    xa = q_a + t_a * x_left + u_a * xb
    xa, xb = xa[None], xb[None]

    for ((u1, t1, _), (u2, t2, _)), (q1, q2) in zip(reversed(tree), reversed(held)):
        xr = q2 + u2 * xa + t2 * xb
        xl = q1 + u1 * xa + t1 * xr
        size = 2 * xa.shape[0]
        xa = jnp.stack([xa, xr], axis=1).reshape(size, depth, width)
        xb = jnp.stack([xl, xb], axis=1).reshape(size, depth, width)
    run_ends[0] = xa
    run_ends[1] = xb

    for side in range(6):
        @pl.when(has[side])
        def _():
            halo(side).wait_send()
    for copy in mat_copies + rhs_copies:
        copy.wait_send()


def finish(res, weight, coef_t, coef_u, coef_q, run_ends, res_hbm, heat_hbm, heat, sem):
    copies = [pltpu.make_async_copy(res, res_hbm, sem.at[2])]
    copies[0].start()
    xa, x = run_ends[0], run_ends[1]
    for i in range(STEPS - 1, -1, -1):
        if i == 0:
            x = xa
        elif i < STEPS - 1:
            x = coef_q[:, i] + coef_u[:, i] * xa + coef_t[:, i] * x
        heat[:, i] = weight[:, i] * x
        if i % 4 == 0:
            part = pl.ds(i, 4)
            copies.append(
                pltpu.make_async_copy(heat.at[:, part], heat_hbm.at[:, part], sem.at[i // 4])
            )
            copies[-1].start()
    for copy in copies:
        copy.wait()


def shards(counts, warmth_field, power_input, inertia_weight, conductivity_lookup, substance_label):
    depth, width = warmth_field.shape[1:]
    shape = (RUNS, STEPS, depth, width)
    vmem = pltpu.VMEM
    whole = vmem(shape, F32)
    others = counts[0] - 1
    dma = pltpu.SemaphoreType.DMA
    hbm_space = pl.BlockSpec(memory_space=pltpu.HBM)
    vmem_space = pl.BlockSpec(memory_space=pltpu.VMEM)
    flat = (RUNS * STEPS * depth, width)
    rows = vmem(flat, F32)
    padded = vmem((flat[0] + 2 * PAD, width), F32)
    held = pl.pallas_call(
        functools.partial(kernel, *counts),
        out_shape=(rows, whole, whole, whole, whole, vmem((2, RUNS, depth, width), F32)),
        in_specs=[hbm_space] * 5,
        out_specs=(vmem_space,) * 6,
        scratch_shapes=[
            padded, whole, vmem(flat, jnp.int32), pltpu.SMEM((8,), F32), padded, whole,
            vmem((2, 2, depth, width), F32), vmem((2, 2, depth, width), F32),
            vmem((2, 2, RUNS * STEPS, width), F32), vmem((2, 2, RUNS * STEPS, width), F32),
            vmem((2, depth, width), F32), vmem((2, 2, depth, width), F32),
            vmem((counts[0], 3, depth, width), F32), vmem((counts[0], 2, depth, width), F32),
            dma((5,)), dma((6,)), dma((6,)),
            dma((others,)), dma((others,)), dma((others,)), dma((others,)),
            pltpu.SemaphoreType.REGULAR,
        ],
        compiler_params=pltpu.CompilerParams(
            collective_id=0, has_side_effects=True, vmem_limit_bytes=32 * 1024 * 1024
        ),
    )(
        *(
            pltpu.with_memory_space_constraint(operand, pltpu.HBM)
            for operand in (
                warmth_field.reshape(flat), power_input.reshape(shape),
                inertia_weight.reshape(shape), conductivity_lookup,
                substance_label.reshape(flat),
            )
        )
    )
    residual, heat_rate = pl.pallas_call(
        finish,
        out_shape=(jax.ShapeDtypeStruct(flat, F32), jax.ShapeDtypeStruct(shape, F32)),
        in_specs=[vmem_space] * 6,
        out_specs=(hbm_space, hbm_space),
        scratch_shapes=[whole, dma((3,))],
    )(*(pltpu.with_memory_space_constraint(array, pltpu.VMEM) for array in held))
    return residual.reshape(warmth_field.shape), heat_rate.reshape(warmth_field.shape)


def solution(mesh):
    counts = tuple(mesh.shape[axis] for axis in ("line", "chip", "layer"))
    spec = P("line", "layer", "chip")
    return jax.shard_map(
        functools.partial(shards, counts),
        mesh=mesh,
        in_specs=(spec, spec, spec, P(), spec),
        out_specs=(spec, spec),
        check_vma=False,
    )
```

```python
import functools

import jax
import jax.numpy as jnp
from jax import lax
from jax.experimental import pallas as pl
from jax.experimental.pallas import tpu as pltpu
from jax.sharding import PartitionSpec as P

MESH = pl.DeviceIdType.MESH
RUNS = 8
STEPS = 8
F32 = jnp.float32


def recip(x):
    return pltpu.reciprocal(x, approx=True)


def conductance(first, second):
    return 2.0 * first * second * recip(first + second)


def eliminate(left, ground, right):
    inv = recip(left + ground + right)
    return left * inv, right * inv, inv


PAD = 8


def spot(run, step, shift=0):
    return pl.ds((run * STEPS + step) * 16 + shift, 16)


def read(ref, step, shift=0):
    return jnp.stack([ref[spot(run, step, shift), :] for run in range(RUNS)])


def write(ref, step, value, shift=0):
    for run in range(RUNS):
        ref[spot(run, step, shift), :] = value[run]


def kernel(
    count_line, count_chip, count_layer,
    temp_hbm, power_hbm, weight_hbm, lut_hbm, label_hbm,
    res, weight, coef_t, coef_u, coef_q, run_ends,
    temp, power, label, lut, cond, gx,
    line_send, line_recv, layer_send, layer_recv, chip_send, chip_recv,
    mats, rights,
    in_sem, halo_send_sem, halo_recv_sem,
    mat_send_sem, mat_recv_sem, rhs_send_sem, rhs_recv_sem, ready_sem,
):
    line = lax.axis_index("line")
    chip = lax.axis_index("chip")
    layer = lax.axis_index("layer")
    depth, width = 16, 128
    rows = RUNS * STEPS

    has = (
        line > 0, line < count_line - 1,
        layer > 0, layer < count_layer - 1,
        chip > 0, chip < count_chip - 1,
    )
    where = (
        {"line": line - 1}, {"line": line + 1},
        {"layer": layer - 1}, {"layer": layer + 1},
        {"chip": chip - 1}, {"chip": chip + 1},
    )
    sends = (line_send, line_send, layer_send, layer_send, chip_send, chip_send)
    recvs = (line_recv, line_recv, layer_recv, layer_recv, chip_recv, chip_recv)

    other = line + 1 - 2 * lax.rem(line, 2)
    offsets = [4, 2, count_line - 2]
    peers = [lax.rem(core + step, count_line) for step in offsets for core in (line, other)] + [other]
    sources = [peers[n] for n in (0, 1, 4, 5, 2, 3, 6)]

    barrier = pltpu.get_barrier_semaphore()
    for side in range(2, 6):
        @pl.when(has[side])
        def _():
            pl.semaphore_signal(barrier, inc=1, device_id=where[side], device_id_type=MESH)
    loads = [
        pltpu.make_async_copy(src, dst, in_sem.at[n])
        for n, (src, dst) in enumerate(
            (
                (label_hbm, label), (temp_hbm, temp.at[pl.ds(PAD, rows * depth)]), (lut_hbm, lut),
                (weight_hbm, weight), (power_hbm, power),
            )
        )
    ]
    for load in loads:
        load.start()

    first_lines = (chip == 0) & (layer == 0)
    other_lines = jnp.logical_not(first_lines)
    greets = [other_lines | ((line > 0) & (peer > 0)) | (line + peer == 1) for peer in peers]
    for n in (6, 2, 3, 4, 5, 0, 1):
        @pl.when(greets[n])
        def _():
            pl.semaphore_signal(barrier, inc=1, device_id={"line": peers[n]}, device_id_type=MESH)


    for side in range(6):
        @pl.when(jnp.logical_not(has[side]))
        def _():
            recvs[side][side % 2] = jnp.zeros(recvs[side].shape[1:], F32)

    def halo(side):
        return pltpu.make_async_remote_copy(
            src_ref=sends[side] if side >= 4 else sends[side].at[side % 2],
            dst_ref=recvs[side].at[1 - side % 2],
            send_sem=halo_send_sem.at[side],
            recv_sem=halo_recv_sem.at[side - side % 2 + 1 - side % 2],
            device_id=where[side],
            device_id_type=MESH,
        )

    def halo_start(side):
        @pl.when(has[side])
        def _():
            halo(side).start()

    def halo_landed(side):
        @pl.when(has[side])
        def _():
            pltpu.make_async_remote_copy(
                src_ref=sends[side] if side >= 4 else sends[side].at[side % 2],
                dst_ref=recvs[side].at[side % 2],
                send_sem=halo_send_sem.at[side],
                recv_sem=halo_recv_sem.at[side],
                device_id=where[side],
                device_id_type=MESH,
            ).wait_recv()

    for ref in (temp, cond):
        for first in (0, rows * depth + PAD):
            ref[pl.ds(first, PAD), :] = jnp.zeros((PAD, width), F32)

    loads[0].wait()
    loads[1].wait()
    x_ends = ((0, 0), (RUNS - 1, STEPS - 1))
    z_ends = (0, depth - 1)
    for end in range(2):
        line_send[end, 0] = temp[spot(*x_ends[end], PAD), :]
        line_send[end, 1] = label[spot(*x_ends[end]), :].astype(F32)
        layer_send[end, 0] = temp[pl.ds(z_ends[end] + PAD, rows, stride=depth), :]
        layer_send[end, 1] = label[pl.ds(z_ends[end], rows, stride=depth), :].astype(F32)

    lane = lax.broadcasted_iota(jnp.int32, (1, 1, width), 2)
    packed = jnp.zeros((RUNS, depth, width), F32)
    for i in range(STEPS):
        packed = jnp.where(
            lane // 2 == 2 * i, pltpu.roll(read(temp, i, PAD), 4 * i + 1, 2),
            jnp.where(
                lane // 2 == 2 * i + 1,
                pltpu.roll(read(label, i).astype(F32), 4 * i + 3, 2),
                packed,
            ),
        )
    packed = packed.reshape(2, 4, depth, width)
    dense = packed[:, 0]
    for k in range(1, 4):
        dense = jnp.where(lane // 32 == k, pltpu.roll(packed[:, k], 32 * k, 2), dense)
    chip_send[...] = dense

    pl.semaphore_wait(barrier, sum(met.astype(jnp.int32) for met in greets + list(has[2:])))
    for side in (2, 3, 4, 5, 0, 1):
        halo_start(side)


    @pl.when(first_lines & (line == 1))
    def _():
        for peer in [peers[n] for n in (6, 0, 1, 2, 3, 4, 5)]:
            pl.semaphore_signal(ready_sem, inc=1, device_id={"line": peer}, device_id_type=MESH)

    loads[2].wait()
    values = [lut[n] for n in range(8)]

    def look_up(tags):
        odd = (tags & 1) == 1
        two = (tags & 2) == 2
        four = tags >= 4
        pairs = [jnp.where(odd, values[2 * n + 1], values[2 * n]) for n in range(4)]
        halves = [jnp.where(two, pairs[2 * n + 1], pairs[2 * n]) for n in range(2)]
        return jnp.where(four, halves[1], halves[0])

    def face_look_up(tags):
        return look_up(tags.astype(jnp.int32))

    for i in range(STEPS):
        write(cond, i, look_up(read(label, i)), PAD)

    for i in range(STEPS - 1):
        gx[:, i] = conductance(read(cond, i, PAD), read(cond, i + 1, PAD))
    k_last, k_first = read(cond, STEPS - 1, PAD), read(cond, 0, PAD)
    join = conductance(k_last, jnp.concatenate([k_first[1:], k_first[:1]], axis=0))
    gx[:, STEPS - 1] = join

    loads[3].wait()
    ya, c, yb = weight[:, 0], gx[:, 0], weight[:, 1]
    for i in range(1, STEPS - 1):
        u, t, inv = eliminate(c, yb, gx[:, i])
        ya = ya + u * yb
        c = c * t
        yb = weight[:, i + 1] + t * yb
        coef_u[:, i] = u
        coef_t[:, i] = t
        coef_q[:, i] = inv
    tree = []
    while ya.shape[0] > 1:
        half = ya.shape[0] // 2
        ya_l, ya_r = (ya.reshape(half, 2, depth, width)[:, n] for n in range(2))
        yb_l, yb_r = (yb.reshape(half, 2, depth, width)[:, n] for n in range(2))
        c_l, c_r = (c.reshape(half, 2, depth, width)[:, n] for n in range(2))
        g, join = (join.reshape(half, 2, depth, width)[:, n] for n in range(2))
        first = eliminate(c_l, yb_l, g)
        u, t, _ = first
        ya = ya_l + u * yb_l
        c = c_l * t
        mid = ya_r + t * yb_l
        second = eliminate(c, mid, c_r)
        u, t, _ = second
        ya = ya + u * mid
        c = c * t
        yb = yb_r + t * mid
        tree.append((first, second))
    ya, c, yb = ya[0], c[0], yb[0]
    t_a, u_a, inv_a = eliminate(2.0 * k_first[0], ya, c)
    y_left, yb, c = t_a * ya, yb + u_a * ya, t_a * c
    u_b, t_b, inv_b = eliminate(c, yb, 2.0 * k_last[RUNS - 1])
    y_left, y_right, c = y_left + u_b * yb, t_b * yb, c * t_b
    mats[line, 0] = y_left
    mats[line, 1] = c
    mats[line, 2] = y_right

    def spread(block, send_sem, recv_sem):
        return [
            pltpu.make_async_remote_copy(
                src_ref=block.at[line],
                dst_ref=block.at[line],
                send_sem=send_sem.at[n],
                recv_sem=recv_sem.at[n],
                device_id={"line": peer},
                device_id_type=MESH,
            )
            for n, peer in enumerate(peers)
        ]

    def landed(block, send_sem, recv_sem):
        for n, source in enumerate(sources):
            pltpu.make_async_remote_copy(
                src_ref=block.at[source],
                dst_ref=block.at[source],
                send_sem=send_sem.at[n],
                recv_sem=recv_sem.at[n],
                device_id={"line": source},
                device_id_type=MESH,
            ).wait_recv()

    mat_copies = spread(mats, mat_send_sem, mat_recv_sem)

    @pl.when(first_lines & (line == 0))
    def _():
        pl.semaphore_wait(ready_sem, 1)

    def start_others(copies):
        @pl.when(other_lines | (line == 0))
        def _():
            for copy in copies:
                copy.start()

        @pl.when(first_lines & (line > 0))
        def _():
            for peer, copy in zip(peers, copies):
                @pl.when(peer > 0)
                def _():
                    copy.start()

    def start_first(block, send_sem, recv_sem):
        n = sum(jnp.where(peer == 0, n, 0) for n, peer in enumerate(peers))

        @pl.when(first_lines & (line > 0))
        def _():
            pltpu.make_async_remote_copy(
                src_ref=block.at[line],
                dst_ref=block.at[line],
                send_sem=send_sem.at[n],
                recv_sem=recv_sem.at[n],
                device_id={"line": 0},
                device_id_type=MESH,
            ).start()

    start_others(mat_copies)

    loads[4].wait()
    row = lax.broadcasted_iota(jnp.int32, (1, depth, 1), 1)
    flow = None
    for i in range(STEPS):
        heat_here, k_here = read(temp, i, PAD), read(cond, i, PAD)
        flow_y = jnp.where(
            lane == width - 1, 0.0,
            conductance(k_here, pltpu.roll(k_here, width - 1, 2))
            * (heat_here - pltpu.roll(heat_here, width - 1, 2)),
        )
        flow_up = jnp.where(
            row == depth - 1, 0.0,
            conductance(k_here, read(cond, i, PAD + 1)) * (heat_here - read(temp, i, PAD + 1)),
        )
        part = power[:, i] - (flow_y - pltpu.roll(flow_y, 1, 2)) - (flow_up - pltpu.roll(flow_up, 1, 1))
        if i < STEPS - 1:
            flow_on = gx[:, i] * (heat_here - read(temp, i + 1, PAD))
        else:
            flow_on = gx[:-1, i] * (heat_here[:-1] - read(temp, 0, PAD)[1:])
            flow_on = jnp.concatenate([flow_on, jnp.zeros((1, depth, width), F32)], axis=0)
        if i > 0:
            part = part + flow
        write(res, i, part - flow_on)
        flow = flow_on
    for run in range(1, RUNS):
        here = spot(run, 0)
        res[here, :] = res[here, :] + flow[run - 1]

    @pl.when(first_lines & (line > 1))
    def _():
        pl.semaphore_wait(ready_sem, 1)

    start_first(mats, mat_send_sem, mat_recv_sem)

    halo_landed(0)
    halo_landed(1)
    for end in range(2):
        here = spot(*x_ends[end])
        g = conductance(cond[spot(*x_ends[end], PAD), :], face_look_up(line_recv[end, 1]))
        g = jnp.where(has[end], g, 0.0)
        res[here, :] = res[here, :] - g * (line_send[end, 0] - line_recv[end, 0])

    own = chip_send[...]
    own_k = face_look_up(pltpu.roll(own, width - 2, 2))
    halo_landed(4)
    halo_landed(5)
    beside = jnp.where(
        lane % 2 == 0, pltpu.roll(chip_recv[1], width - 1, 2), pltpu.roll(chip_recv[0], 1, 2)
    )
    beside_k = face_look_up(pltpu.roll(beside, width - 2, 2))
    open_lane = ((lane % 4 == 0) & has[5]) | ((lane % 4 == 1) & has[4])
    edge = jnp.where(open_lane, conductance(own_k, beside_k) * (own - beside), 0.0)
    edges = jnp.stack(
        [edge] + [pltpu.roll(edge, width - 32 * k, 2) for k in range(1, 4)], axis=1
    ).reshape(RUNS, depth, width)
    at_edge = (lane == 0) | (lane == width - 1)
    for i in range(STEPS):
        write(res, i, read(res, i) - jnp.where(
            at_edge, pltpu.roll(edges, width - 1 - 4 * i, 2), 0.0
        ))

    is_top = layer == count_layer - 1
    own_faces = [cond[pl.ds(first + PAD, rows, stride=depth), :] for first in z_ends]
    halo_landed(2)
    halo_landed(3)
    for end in range(2):
        face = pl.ds(z_ends[end], rows, stride=depth)
        own_k = own_faces[end]
        g = conductance(own_k, face_look_up(layer_recv[end, 1]))
        if end == 0:
            g = jnp.where(has[2], g, 0.0)
        else:
            g = jnp.where(is_top, own_k, g)
        res[face, :] = res[face, :] - g * (layer_send[end, 0] - layer_recv[end, 0])
    for i in range(STEPS):
        right = read(res, i).astype(jnp.bfloat16).astype(F32)
        if i == 0:
            ra = right
        elif i == 1:
            rb = right
        else:
            ra = ra + coef_u[:, i - 1] * rb
            held = coef_t[:, i - 1] * rb
            coef_q[:, i - 1] = coef_q[:, i - 1] * rb
            rb = right + held

    held = []
    for (u1, t1, inv1), (u2, t2, inv2) in tree:
        half = ra.shape[0] // 2
        ra_l, ra_r = (ra.reshape(half, 2, depth, width)[:, n] for n in range(2))
        rb_l, rb_r = (rb.reshape(half, 2, depth, width)[:, n] for n in range(2))
        mid = ra_r + t1 * rb_l
        held.append((inv1 * rb_l, inv2 * mid))
        ra = ra_l + u1 * rb_l + u2 * mid
        rb = rb_r + t2 * mid
    ra, rb = ra[0], rb[0]
    rb = rb + u_a * ra
    r_left, r_right = t_a * ra + u_b * rb, t_b * rb
    rights[line, 0] = r_left
    rights[line, 1] = r_right
    rhs_copies = spread(rights, rhs_send_sem, rhs_recv_sem)
    start_others(rhs_copies)

    start_first(rights, rhs_send_sem, rhs_recv_sem)
    q_a, q_b = inv_a * ra, inv_b * rb

    landed(mats, mat_send_sem, mat_recv_sem)
    zero = jnp.zeros((depth, width), F32)
    before, after = zero, zero
    up, down = [], []
    for j in range(count_line - 1):
        a = before + mats[j, 0]
        u = mats[j, 1] * recip(a + mats[j, 1])
        before = jnp.where(j < line, mats[j, 2] + u * a, before)
        up.append(u)
        n = count_line - 1 - j
        a = after + mats[n, 2]
        u = mats[n, 1] * recip(a + mats[n, 1])
        after = jnp.where(n > line, mats[n, 0] + u * a, after)
        down.append(u)
    a = y_left + before
    b = y_right + after
    inv = recip(a * b + c * (a + b))
    from_a, from_b, cross = (b + c) * inv, (a + c) * inv, c * inv

    landed(rights, rhs_send_sem, rhs_recv_sem)
    left_in, right_in = zero, zero
    for j in range(count_line - 1):
        new = rights[j, 1] + up[j] * (rights[j, 0] + left_in)
        left_in = jnp.where(j < line, new, left_in)
        n = count_line - 1 - j
        new = rights[n, 0] + down[j] * (rights[n, 1] + right_in)
        right_in = jnp.where(n > line, new, right_in)
    left_in = left_in + r_left
    right_in = right_in + r_right
    x_left = from_a * left_in + cross * right_in
    x_right = cross * left_in + from_b * right_in
    xb = q_b + u_b * x_left + t_b * x_right
    xa = q_a + t_a * x_left + u_a * xb
    xa, xb = xa[None], xb[None]

    for ((u1, t1, _), (u2, t2, _)), (q1, q2) in zip(reversed(tree), reversed(held)):
        xr = q2 + u2 * xa + t2 * xb
        xl = q1 + u1 * xa + t1 * xr
        size = 2 * xa.shape[0]
        xa = jnp.stack([xa, xr], axis=1).reshape(size, depth, width)
        xb = jnp.stack([xl, xb], axis=1).reshape(size, depth, width)
    run_ends[0] = xa
    run_ends[1] = xb

    for side in range(6):
        @pl.when(has[side])
        def _():
            halo(side).wait_send()
    for copy in mat_copies + rhs_copies:
        copy.wait_send()


def finish(res, weight, coef_t, coef_u, coef_q, run_ends, res_hbm, heat_hbm, heat, sem):
    copies = [pltpu.make_async_copy(res, res_hbm, sem.at[4])]
    copies[0].start()
    xa, x = run_ends[0], run_ends[1]
    for i in range(STEPS - 1, -1, -1):
        if i == 0:
            x = xa
        elif i < STEPS - 1:
            x = coef_q[:, i] + coef_u[:, i] * xa + coef_t[:, i] * x
        heat[:, i] = weight[:, i] * x
        if i % 2 == 0:
            part = pl.ds(i, 2)
            copies.append(
                pltpu.make_async_copy(heat.at[:, part], heat_hbm.at[:, part], sem.at[i // 2])
            )
            copies[-1].start()
    for copy in copies:
        copy.wait()


def shards(counts, warmth_field, power_input, inertia_weight, conductivity_lookup, substance_label):
    depth, width = warmth_field.shape[1:]
    shape = (RUNS, STEPS, depth, width)
    vmem = pltpu.VMEM
    whole = vmem(shape, F32)
    others = counts[0] - 1
    dma = pltpu.SemaphoreType.DMA
    hbm_space = pl.BlockSpec(memory_space=pltpu.HBM)
    vmem_space = pl.BlockSpec(memory_space=pltpu.VMEM)
    flat = (RUNS * STEPS * depth, width)
    rows = vmem(flat, F32)
    padded = vmem((flat[0] + 2 * PAD, width), F32)
    held = pl.pallas_call(
        functools.partial(kernel, *counts),
        out_shape=(rows, whole, whole, whole, whole, vmem((2, RUNS, depth, width), F32)),
        in_specs=[hbm_space] * 5,
        out_specs=(vmem_space,) * 6,
        scratch_shapes=[
            padded, whole, vmem(flat, jnp.int32), pltpu.SMEM((8,), F32), padded, whole,
            vmem((2, 2, depth, width), F32), vmem((2, 2, depth, width), F32),
            vmem((2, 2, RUNS * STEPS, width), F32), vmem((2, 2, RUNS * STEPS, width), F32),
            vmem((2, depth, width), F32), vmem((2, 2, depth, width), F32),
            vmem((counts[0], 3, depth, width), F32), vmem((counts[0], 2, depth, width), F32),
            dma((5,)), dma((6,)), dma((6,)),
            dma((others,)), dma((others,)), dma((others,)), dma((others,)),
            pltpu.SemaphoreType.REGULAR,
        ],
        compiler_params=pltpu.CompilerParams(
            collective_id=0, has_side_effects=True, vmem_limit_bytes=32 * 1024 * 1024
        ),
    )(
        *(
            pltpu.with_memory_space_constraint(operand, pltpu.HBM)
            for operand in (
                warmth_field.reshape(flat), power_input.reshape(shape),
                inertia_weight.reshape(shape), conductivity_lookup,
                substance_label.reshape(flat),
            )
        )
    )
    residual, heat_rate = pl.pallas_call(
        finish,
        out_shape=(jax.ShapeDtypeStruct(flat, F32), jax.ShapeDtypeStruct(shape, F32)),
        in_specs=[vmem_space] * 6,
        out_specs=(hbm_space, hbm_space),
        scratch_shapes=[whole, dma((5,))],
    )(*(pltpu.with_memory_space_constraint(array, pltpu.VMEM) for array in held))
    return residual.reshape(warmth_field.shape), heat_rate.reshape(warmth_field.shape)


def solution(mesh):
    counts = tuple(mesh.shape[axis] for axis in ("line", "chip", "layer"))
    spec = P("line", "layer", "chip")
    return jax.shard_map(
        functools.partial(shards, counts),
        mesh=mesh,
        in_specs=(spec, spec, spec, P(), spec),
        out_specs=(spec, spec),
        check_vma=False,
    )
```
